768 devices in a mesh: ctx: 64 (over x, y, core), tp: 12 (over z).
Axes of the slice: x: 4, y: 8, z: 12, core: 2. Of those that a mesh axis runs over, the one named last changes fastest.
Arguments:
- tokens: bfloat16 [98304, 2048], P(('ctx', 'tp')), may hold values from -8 to 8
- projection: bfloat16 [2048, 1920], P(None, 'tp'), may hold values from -0.125 to 0.125
- conv_weight: float32 [4, 1920], P(None, 'tp'), may hold values from -2.5 to 2.5
Outputs:
- attended: bfloat16 [98304, 1536], P('ctx', 'tp')
The draws below stay inside these ranges and needn't reach their ends.
All inputs are finite; a program needn't handle non-finite values.
Results may differ from the reference program's by a relative error of at most 0.0032.
The reference program's roundings to bfloat16 on the way (of `projected` and `values`) count: a program that leaves them out, or rounds other values in their place, can miss the bound.
Values may be sent and summed in bfloat16 or wider, within the bound.
A program may use at most 64 MiB of HBM per device.

```python
import math
import jax
import jax.numpy as jnp
from jax import lax

D = 2048
FEAT = 16
VW = 128
KERNEL = 4
HEADS = 12
PHI = 273
BLOCK = 768
TOKENS = 98304


def draw_tokens(key, part):
    key_noise, key_segment, key_common = jax.random.split(jax.random.fold_in(key, 7), 3)
    seg_len = 16
    noise = jnp.clip(jax.random.normal(key_noise, (TOKENS, D), jnp.float32), -4.0, 4.0)
    segment_mean = 0.8 * jnp.clip(jax.random.normal(key_segment, (TOKENS // seg_len, D), jnp.float32), -3.0, 3.0)
    common_mean = 0.5 * jnp.clip(jax.random.normal(key_common, (1, D), jnp.float32), -2.0, 2.0)
    values = noise + jnp.repeat(segment_mean, seg_len, axis=0) + common_mean
    return jnp.clip(values, -8.0, 8.0).astype(jnp.bfloat16)


def level_of(own_key, extent, shards, low, top_value):
    def one(position, blocks):
        steps = jax.random.uniform(jax.random.fold_in(jax.random.fold_in(own_key, 6), position), (blocks,), jnp.float32, low / len(shards), top_value / len(shards))
        return jnp.repeat(jnp.exp(steps), extent[position] // blocks).reshape((-1,) + (1,) * (len(extent) - position - 1))

    gain = one(*shards[0])
    for cut in shards[1:]:
        gain = gain * one(*cut)
    return gain


def gaussian(own_key, extent, scale, limit, cuts=(), dtype=jnp.bfloat16):
    array = scale * jax.random.normal(own_key, extent, jnp.float32)
    if cuts:
        array = array * level_of(own_key, extent, cuts, -0.22, 0.18)
    return jnp.clip(array, -limit, limit).astype(dtype)


def setup_inputs(seed: int = 0) -> dict:
    streams_of = jax.random.split(jax.random.key(seed), 4)
    tokens = draw_tokens(jax.random.fold_in(streams_of[3], 71), 0)
    projection = gaussian(streams_of[1], (D, HEADS * (2 * FEAT + VW)), D ** -0.5, 0.125, ((1, 12),))
    conv_weight = gaussian(streams_of[2], (KERNEL, HEADS * (2 * FEAT + VW)), 0.5, 2.5, ((1, 12),), jnp.float32)
    return dict(tokens=tokens, projection=projection, conv_weight=conv_weight)


def taylor(raw_vals):
    width_feat = raw_vals.shape[-1]
    linear = raw_vals * width_feat ** (-0.25)
    quadratic = raw_vals[..., :, None] * raw_vals[..., None, :]
    quadratic = quadratic.reshape(raw_vals.shape[:-1] + (width_feat * width_feat,))
    quadratic = quadratic * (1.0 / (math.sqrt(2.0) * math.sqrt(width_feat)))
    ones_col = jnp.ones(raw_vals.shape[:-1] + (1,), jnp.float32)
    return jnp.concatenate([ones_col, linear, quadratic], axis=-1).astype(jnp.bfloat16)

def reference(tokens, projection, conv_weight):
    row_width = 2 * FEAT + VW
    conv_lag = KERNEL - 1
    num_blocks = TOKENS // BLOCK
    token_blocks = tokens.reshape(num_blocks, BLOCK, D)
    causal = jnp.arange(BLOCK)[:, None] >= jnp.arange(BLOCK)[None, :]
    highest = lax.Precision.HIGHEST

    def block_step(carried, block_rows):
        tail_rows, run_state, run_total = carried
        projected = jnp.dot(block_rows, projection, preferred_element_type=jnp.float32).astype(jnp.bfloat16)
        padded = jnp.concatenate([tail_rows, projected], axis=0).astype(jnp.float32)
        convolved = jnp.zeros((BLOCK, HEADS * row_width), jnp.float32)
        for offset in range(KERNEL):
            convolved = convolved + conv_weight[offset] * padded[conv_lag - offset:conv_lag - offset + BLOCK]
        convolved = convolved.reshape(BLOCK, HEADS, row_width)
        feat_query = taylor(convolved[:, :, :FEAT]).astype(jnp.float32)
        feat_key = taylor(convolved[:, :, FEAT:2 * FEAT]).astype(jnp.float32)
        values = convolved[:, :, 2 * FEAT:].astype(jnp.bfloat16).astype(jnp.float32)
        scores = jnp.einsum('ihp,jhp->hij', feat_query, feat_key, precision=highest)
        scores = jnp.where(causal[None], scores, jnp.float32(0.0))
        rounded = lax.optimization_barrier(scores.astype(jnp.bfloat16)).astype(jnp.float32)
        numerator = jnp.einsum('hij,jhv->ihv', rounded, values, precision=highest)
        denominator = jnp.transpose(lax.optimization_barrier(jnp.sum(scores, axis=2)))
        numerator = numerator + jnp.einsum('ihp,hpv->ihv', feat_query, run_state, precision=highest)
        denominator = denominator + jnp.einsum('ihp,hp->ih', feat_query, run_total, precision=highest)
        run_state = run_state + jnp.einsum('jhp,jhv->hpv', feat_key, values, precision=highest)
        run_total = run_total + lax.optimization_barrier(jnp.sum(feat_key, axis=0))
        attended = (numerator / denominator[:, :, None]).astype(jnp.bfloat16).reshape(BLOCK, HEADS * VW)
        return ((projected[BLOCK - conv_lag:], run_state, run_total), attended)
    initial = (jnp.zeros((conv_lag, HEADS * row_width), jnp.bfloat16), jnp.zeros((HEADS, PHI, VW), jnp.float32), jnp.zeros((HEADS, PHI), jnp.float32))
    _, outputs = lax.scan(block_step, initial, token_blocks)
    return outputs.reshape(TOKENS, HEADS * VW)
```

```python
import jax
import jax.numpy as jnp
from jax import lax
from jax.experimental import pallas as pl
from jax.experimental.pallas import tpu as pltpu
from jax.sharding import PartitionSpec as P

NX, NY, NZ = 4, 8, 12
D = 2048
FEAT = 16
VW = 128
TILE = 128
ROWS = TILE * NZ
PACK = TILE // 4
PHI = 160
HALF = PHI // 2
TOT = 153
BLOCK = 768
SUB = 256
MESH = pl.DeviceIdType.MESH
bf16, f32 = jnp.bfloat16, jnp.float32


def kernel(tok_ref, proj_ref, conv_ref, out_ref,
           tokbuf, sa, sb, wa, wb, stage, xr, vb, fq, fk, st, loc, px, ch, ybuf, tx, xbuf, snd, fin, num, den,
           tk_s, tk_r, zs, zr, xs_s, xs_r, ya_s, ya_r, yb_s, yb_r, xb_s, xb_r, at_s, at_r, h_s, h_r,
           d1_s, d1_r, sy_s, sy_r, sx_s, sx_r, d2_s, d2_r):
    c = lax.axis_index("ctx")
    z = lax.axis_index("tp")
    r = lax.rem(c, 2)
    y = lax.rem(c // 2, NY)
    x = c // (2 * NY)

    def at(xx, yy, rr, zz):
        return ((xx * NY + yy) * 2 + rr, zz)

    def xo(d):
        return lax.rem(x + d + NX, NX)

    def yo(d):
        return lax.rem(y + d + NY, NY)

    def zo(d):
        return lax.rem(z + d + NZ, NZ)

    def copy(src, dst, ss, rs, dev):
        return pltpu.make_async_remote_copy(
            src_ref=src, dst_ref=dst, send_sem=ss, recv_sem=rs, device_id=dev, device_id_type=MESH)

    barrier = pltpu.get_barrier_semaphore()

    def greet(dev):
        pl.semaphore_signal(barrier, inc=1, device_id=dev, device_id_type=MESH)

    greet(at(x, y, 1 - r, z))
    for d in range(1, NX):
        greet(at(xo(d), y, r, z))
    for d in range(1, NY):
        greet(at(x, yo(d), r, z))
    for d in range(1, NZ):
        greet(at(x, y, r, zo(d)))
        greet(at(x, y, 1 - r, zo(d)))
    halo_in = jnp.logical_and(r == 0, c > 0)

    @pl.when(halo_in)
    def _():
        greet((c - 1, z))

    def value_rows(start, n):
        a = proj_ref[pl.ds(pl.multiple_of(start, 16), n), 0:128]
        b = proj_ref[pl.ds(pl.multiple_of(start, 16), n), 128:160]
        return jnp.concatenate([a[:, 32:], b], axis=1)

    def packed_rows(start, n):
        return jnp.concatenate(
            [proj_ref[pl.ds(pl.multiple_of(j * 512 + start, 16), n), 0:32] for j in range(4)], axis=1)

    for g in range(4):
        sa[g] = value_rows(y * 256 + g * 64 + x * 16, 16)
    sa[4] = packed_rows(y * 64 + x * 16, 16)
    ypar = lax.rem(y, 2)
    for g in range(4):
        sb[g] = value_rows(x * 512 + g * 128 + ypar * 64, 64)
    sb[4] = packed_rows(x * 128 + ypar * 64, 64)
    own_rows = pl.ds(pl.multiple_of(r * TILE, TILE), TILE)
    tokbuf[own_rows, :] = tok_ref[...]

    pl.semaphore_wait(barrier, NX + NY - 1 + 2 * (NZ - 1) + r * (1 - c // (2 * NX * NY - 1)))

    sends = []

    def dist(k):
        return jnp.where(r == 0, 6 - k, k - 6 if k else 0)

    xpiece = pl.ds(pl.multiple_of(x * 16, 16), 16)
    ypiece = pl.ds(pl.multiple_of(ypar * 64, 64), 64)

    def z_copy(k):
        i = k // 2
        dev = at(x, y, r, zo(-dist(k)))
        if k % 2 == 0:
            return copy(sa, wa.at[i, y, :, xpiece, :], zs.at[k], zr.at[k], dev)
        return copy(sb, wb.at[i, x, :, ypiece, :], zs.at[k], zr.at[k], dev)

    tok_copy = copy(tok_ref, tokbuf.at[own_rows, :], tk_s, tk_r, at(x, y, 1 - r, z))
    z_copies = [z_copy(k) for k in range(6)]

    @pl.when(r == 0)
    def _():
        z_copies[0].start()

    @pl.when(r == 1)
    def _():
        wa[0, y, :, xpiece, :] = sa[...]

    for k in range(1, 6):
        z_copies[k].start()
    tok_copy.start()
    sends.append(tok_copy)
    sends.extend(z_copies[1:])

    xs = {}
    pair = {}
    ring = {}
    xb = {}

    def a_small(i):
        if i == 0:
            @pl.when(r == 0)
            def _():
                z_copies[0].wait_recv()
        else:
            z_copies[2 * i].wait_recv()
        for d in range(1, NX):
            ref = wa.at[i, y, :, xpiece, :]
            cp = copy(ref, ref, xs_s.at[i, d - 1], xs_r.at[i, d - 1], at(xo(d), y, r, z))
            cp.start()
            xs[i, d] = cp
            sends.append(cp)

    def b_small(i):
        z_copies[2 * i + 1].wait_recv()
        ref = wb.at[i, x, :, ypiece, :]
        cp = copy(ref, ref, yb_s.at[i], yb_r.at[i], at(x, y + 1 - 2 * ypar, r, z))
        cp.start()
        pair[i] = cp
        sends.append(cp)

    def b_large(i):
        pair[i].wait_recv()
        for d in range(1, NX):
            ref = wb.at[i, x]
            cp = copy(ref, ref, xb_s.at[i, d - 1], xb_r.at[i, d - 1], at(xo(d), y, r, z))
            cp.start()
            xb[i, d] = cp
            sends.append(cp)

    def a_ring(i, s):
        if s == 1:
            for d in range(1, NX):
                xs[i, d].wait_recv()
        else:
            ring[i, 0, s - 1].wait_recv()
            ring[i, 1, s - 1].wait_recv()
        for way, sign in ((0, 1), (1, -1)):
            part = slice(None) if s < 4 else pl.ds(32 * way, 32)
            ref = wa.at[i, yo(-sign * (s - 1)), :, part, :]
            cp = copy(ref, ref, ya_s.at[i, way, s - 1], ya_r.at[i, way, s - 1], at(x, yo(sign), r, z))
            cp.start()
            ring[i, way, s] = cp
            sends.append(cp)

    lane = lax.broadcasted_iota(jnp.int32, (SUB, 128), 1) // 32

    def project(k):
        i = k // 2
        v = jnp.zeros((2 * TILE, 128), f32)
        q = jnp.zeros((2 * TILE, 128), f32)
        for j in range(4):
            if k % 2 == 0:
                w = jnp.concatenate([wa[i, 2 * j, 0:4].reshape(256, 128),
                                     wa[i, 2 * j + 1, 0:4].reshape(256, 128)], axis=0)
                p = wa[i, :, 4].reshape(512, 128)
            else:
                w = wb[i, j, 0:4].reshape(512, 128)
                p = wb[i, :, 4].reshape(512, 128)
            t = jnp.dot(tokbuf[:, j * 512:(j + 1) * 512], jnp.concatenate([w, p], axis=1),
                        preferred_element_type=f32)
            v = v + t[:, :128]
            q = q + jnp.where(lane == j, t[:, 128:], 0.0)
        q = q + pltpu.roll(q, 64, 1)
        q = q + pltpu.roll(q, 32, 1)
        for b in range(2):
            stage[k, b, 0:TILE, :] = v[b * TILE:(b + 1) * TILE].astype(bf16)
            rows = q[b * TILE:(b + 1) * TILE].reshape(4, PACK, 128)
            pk = rows[0]
            for j in range(1, 4):
                pk = jnp.where(lane[:PACK] == j, rows[j], pk)
            stage[k, b, TILE:, :] = pk.astype(bf16)

    tile_copies = {}

    def scatter(k):
        for b in range(2):
            cp = copy(stage.at[k, b], xr.at[z + 1], at_s.at[k, b], at_r.at[z], at(x, y, b, zo(dist(k))))
            tile_copies[k, b] = cp
            if k == 0 and b == 1:
                @pl.when(r == 0)
                def _():
                    cp.start()

                @pl.when(r == 1)
                def _():
                    xr[z + 1] = stage[0, 1]
            else:
                cp.start()

    a_small(0)
    b_small(0)
    a_small(1)
    b_small(1)
    a_ring(0, 1)
    b_large(0)
    a_small(2)
    b_small(2)
    a_ring(1, 1)
    b_large(1)
    a_ring(0, 2)
    a_ring(2, 1)
    b_large(2)
    a_ring(1, 2)
    a_ring(0, 3)
    a_ring(2, 2)
    a_ring(1, 3)
    a_ring(0, 4)
    tok_copy.wait_recv()

    def finish_b(i):
        for d in range(1, NX):
            xb[i, d].wait_recv()
        project(2 * i + 1)
        scatter(2 * i + 1)

    def finish_a(i):
        ring[i, 0, 4].wait_recv()
        ring[i, 1, 4].wait_recv()
        project(2 * i)
        scatter(2 * i)

    finish_b(0)
    a_ring(2, 3)
    finish_a(0)
    a_ring(1, 4)
    finish_b(1)
    a_ring(2, 4)
    finish_a(1)
    finish_b(2)
    finish_a(2)

    def await_tile(t):
        copy(stage.at[0, 0], xr.at[t + 1], at_s.at[0, 0], at_r.at[t], at(x, y, r, z)).wait_recv()

    last = NZ - 1

    def tile_in(t):
        @pl.when(jnp.logical_or(r == 0, z != t))
        def _():
            await_tile(t)

    tile_in(last)

    def halo(n):
        rows = pl.ds(112 + 32 * n, 16)
        return copy(xr.at[NZ, rows, :], xr.at[0, rows, :], h_s.at[n], h_r.at[n], (c + 1, z))

    @pl.when(c < 2 * NX * NY - 1)
    def _():
        halo(0).start()
        halo(1).start()

    for t in range(last):
        tile_in(t)

    @pl.when(c == 0)
    def _():
        xr[0, 112:128] = jnp.zeros((16, 128), bf16)
        xr[0, 144:160] = jnp.zeros((16, 128), bf16)

    @pl.when(c > 0)
    def _():
        for n in range(2):
            rows = pl.ds(112 + 32 * n, 16)
            copy(xr.at[NZ, rows, :], xr.at[0, rows, :], h_s.at[n], h_r.at[n], (c - 1, z)).wait_recv()

    ca = conv_ref[:, 0:128]
    cb = conv_ref[:, 128:160]
    cv = jnp.concatenate([ca[:, 32:], cb], axis=1)
    cqk = jnp.concatenate([ca[:, :32]] * 4, axis=1)
    plane = lax.broadcasted_iota(jnp.int32, (PACK, 128), 1)
    quad = 1.0 / (2.0 ** 0.5 * FEAT ** 0.5)
    one_row = jnp.where(lax.broadcasted_iota(jnp.int32, (8, 128), 0) == 0, 1.0, 0.0)

    def features(u, twice):
        parts = [u * u * quad]
        for d in range(1, 8):
            parts.append(u * pltpu.roll(u, FEAT - d, 0) * (quad * twice))
        parts.append((u * pltpu.roll(u, 8, 0) * (quad * twice))[:8])
        parts.append(u * FEAT ** -0.25)
        parts.append(one_row)
        return jnp.concatenate(parts, axis=0)

    @pl.loop(0, NZ)
    def _(t):
        before = xr[t, 112:128].astype(f32)
        now = xr[t + 1, 0:TILE].astype(f32)
        window = jnp.concatenate([before[8:], now], axis=0)
        acc = jnp.zeros((TILE, 128), f32)
        for o in range(4):
            acc = acc + cv[o:o + 1] * window[8 - o:8 - o + TILE]
        rows = pl.ds(pl.multiple_of(t * TILE, TILE), TILE)
        vb[rows, :] = acc.astype(bf16)
        pk = xr[t + 1, TILE:].astype(f32)
        before = xr[t, 144:160].astype(f32)
        edge = jnp.where(plane[:8] < 32, pltpu.roll(before[8:], 32, 1), pltpu.roll(pk[24:], 32, 1))
        window = jnp.concatenate([edge, pk], axis=0)
        qk = jnp.zeros((PACK, 128), f32)
        for o in range(4):
            qk = qk + cqk[o:o + 1] * window[8 - o:8 - o + PACK]
        wide = jnp.concatenate([qk] + [pltpu.roll(qk, 128 - 32 * j, 1) for j in range(1, 4)], axis=0)
        tall = wide.T
        fq[rows, :] = features(tall[0:FEAT], 2.0).T.astype(bf16)
        fk[t] = features(tall[FEAT:2 * FEAT], 1.0).astype(bf16)

    per = BLOCK // TILE
    ones = jnp.ones((8, BLOCK), bf16)
    for b in range(2):
        keys = jnp.concatenate([fk[b * per + t] for t in range(per)], axis=1)
        st[b] = jnp.dot(keys, vb[b * BLOCK:(b + 1) * BLOCK, :], preferred_element_type=f32)
        total = lax.dot_general(ones, keys, (((1,), (1,)), ((), ())), preferred_element_type=f32)
        st[b, TOT:TOT + 1, :] = total[0:1, 0:128]
        st[b, TOT + 1:TOT + 2, 0:32] = total[0:1, 128:160]
    loc[...] = st[0] + st[1]

    mine = pl.ds(pl.multiple_of(r * HALF, 8), HALF)
    other = pl.ds(pl.multiple_of((1 - r) * HALF, 8), HALF)
    partner = at(x, y, 1 - r, z)
    d1 = copy(loc.at[other, :], px, d1_s, d1_r, partner)
    d1.start()
    sends.append(d1)

    def within(b):
        for i in range(BLOCK // SUB):
            cols = (i + 1) * SUB
            keys = jnp.concatenate([fk[b * per + t] for t in range(cols // TILE)], axis=1)
            row = b * BLOCK + i * SUB
            w = jnp.dot(fq[row:row + SUB, :], keys, preferred_element_type=f32)
            causal = (lax.broadcasted_iota(jnp.int32, (SUB, cols), 0) + i * SUB
                      >= lax.broadcasted_iota(jnp.int32, (SUB, cols), 1))
            w = jnp.where(causal, w, 0.0)
            num[row:row + SUB, :] = jnp.dot(w.astype(bf16), vb[b * BLOCK:b * BLOCK + cols, :],
                                            preferred_element_type=f32)
            den[row:row + SUB, :] = jnp.broadcast_to(jnp.sum(w, axis=1, keepdims=True), (SUB, 128))

    d1.wait_recv()
    ch[...] = loc[mine, :] + px[...]
    sy = []
    for d in range(1, NY):
        cp = copy(ch, ybuf.at[d - 1], sy_s.at[d - 1], sy_r.at[d - 1], at(x, yo(d), r, z))
        cp.start()
        sy.append(cp)
    sends.extend(sy)
    within(0)
    within(1)
    total = ch[...]
    before = jnp.zeros((HALF, 128), f32)
    for d in range(1, NY):
        sy[d - 1].wait_recv()
        got = ybuf[d - 1]
        total = total + got
        before = before + jnp.where(y >= d, got, 0.0)
    tx[...] = total
    sx = []
    for d in range(1, NX):
        cp = copy(tx, xbuf.at[d - 1], sx_s.at[d - 1], sx_r.at[d - 1], at(xo(d), y, r, z))
        cp.start()
        sx.append(cp)
    sends.extend(sx)
    for d in range(1, NX):
        sx[d - 1].wait_recv()
        before = before + jnp.where(x >= d, xbuf[d - 1], 0.0)
    snd[...] = before + jnp.where(r == 0, loc[mine, :], 0.0)
    d2 = copy(snd, fin.at[mine, :], d2_s, d2_r, partner)
    d2.start()
    sends.append(d2)
    fin[mine, :] = before + jnp.where(r == 1, px[...], 0.0)
    d2.wait_recv()

    for b in range(2):
        state = fin[...] if b == 0 else fin[...] + st[0]
        high = state.astype(bf16)
        low = (state - high.astype(f32)).astype(bf16)
        row = jnp.concatenate([state[TOT:TOT + 1, :], state[TOT + 1:TOT + 2, 0:32]], axis=1)
        row_high = row.astype(bf16).astype(f32)
        which = lax.broadcasted_iota(jnp.int32, (16, PHI), 0)
        rows = jnp.where(which == 0, row_high, jnp.where(which == 1, row - row_high, 0.0)).astype(bf16)
        for i in range(BLOCK // SUB):
            at_rows = slice(b * BLOCK + i * SUB, b * BLOCK + (i + 1) * SUB)
            f = fq[at_rows, :]
            top = num[at_rows, :] + jnp.dot(f, high, preferred_element_type=f32)
            top = top + jnp.dot(f, low, preferred_element_type=f32)
            two = lax.dot_general(f, rows, (((1,), (1,)), ((), ())), preferred_element_type=f32)
            bottom = den[at_rows, :] + (two[:, 0:1] + two[:, 1:2])
            out_ref[at_rows, :] = (top / bottom).astype(bf16)

    @pl.when(r == 0)
    def _():
        z_copies[0].wait_send()
        tile_copies[0, 1].wait_send()

    for (k, b), cp in tile_copies.items():
        if (k, b) != (0, 1):
            cp.wait_send()
    for cp in sends:
        cp.wait_send()

    @pl.when(c < 2 * NX * NY - 1)
    def _():
        halo(0).wait_send()
        halo(1).wait_send()


def per_device(tokens, projection, conv_weight):
    vmem = pltpu.VMEM
    dma = pltpu.SemaphoreType.DMA
    return pl.pallas_call(
        kernel,
        out_shape=jax.ShapeDtypeStruct((ROWS, VW), bf16),
        in_specs=[pl.BlockSpec(memory_space=vmem)] * 3,
        out_specs=pl.BlockSpec(memory_space=vmem),
        scratch_shapes=[
            vmem((2 * TILE, D), bf16),
            vmem((5, 16, 128), bf16),
            vmem((5, 64, 128), bf16),
            vmem((3, NY, 5, 64, 128), bf16),
            vmem((3, NX, 5, 128, 128), bf16),
            vmem((6, 2, TILE + PACK, 128), bf16),
            vmem((NZ + 1, TILE + PACK, 128), bf16),
            vmem((ROWS, VW), bf16),
            vmem((ROWS, PHI), bf16),
            vmem((NZ, PHI, TILE), bf16),
            vmem((2, PHI, 128), f32),
            vmem((PHI, 128), f32),
            vmem((HALF, 128), f32),
            vmem((HALF, 128), f32),
            vmem((NY - 1, HALF, 128), f32),
            vmem((HALF, 128), f32),
            vmem((NX - 1, HALF, 128), f32),
            vmem((HALF, 128), f32),
            vmem((PHI, 128), f32),
            vmem((ROWS, 128), f32),
            vmem((ROWS, 128), f32),
            dma, dma,
            dma((6,)), dma((6,)),
            dma((3, NX - 1)), dma((3, NX - 1)),
            dma((3, 2, 4)), dma((3, 2, 4)),
            dma((3,)), dma((3,)),
            dma((3, NX - 1)), dma((3, NX - 1)),
            dma((6, 2)), dma((NZ,)),
            dma((2,)), dma((2,)),
            dma, dma,
            dma((NY - 1,)), dma((NY - 1,)),
            dma((NX - 1,)), dma((NX - 1,)),
            dma, dma,
        ],
        compiler_params=pltpu.CompilerParams(
            collective_id=0, has_side_effects=True, vmem_limit_bytes=48 * 2**20),
        name="fused",
    )(tokens, projection, conv_weight)


def solution(mesh):
    return jax.shard_map(
        per_device,
        mesh=mesh,
        in_specs=(P(("ctx", "tp"), None), P(None, "tp"), P(None, "tp")),
        out_specs=P("ctx", "tp"),
        check_vma=False,
    )
```

```python
import jax
import jax.numpy as jnp
from jax import lax
from jax.experimental import pallas as pl
from jax.experimental.pallas import tpu as pltpu
from jax.sharding import PartitionSpec as P

NX, NY, NZ = 4, 8, 12
D = 2048
FEAT = 16
VW = 128
WIDTH = 2 * FEAT + VW
TILE = 128
ROWS = TILE * NZ
PHI = 160
HALF = PHI // 2
TOT = 153
BLOCK = 768
SUB = 256
MESH = pl.DeviceIdType.MESH
bf16, f32 = jnp.bfloat16, jnp.float32


def dot_nt(a, b):
    return lax.dot_general(a, b, (((1,), (1,)), ((), ())), preferred_element_type=f32)


def kernel(tok_ref, proj_ref, conv_ref, out_ref,
           tokbuf, wr, wx, stage, xr, cw, vt, fq, fk, st, loc, px, ch, ybuf, tx, xbuf, snd, fin, num, den,
           tk_s, tk_r, zr_s, zr_r, zx_s, zx_r, xs_s, xs_r, ya_s, ya_r, yb_s, yb_r, xb_s, xb_r, at_s, at_r, h_s, h_r,
           d1_s, d1_r, sy_s, sy_r, sx_s, sx_r, d2_s, d2_r):
    c = lax.axis_index("ctx")
    z = lax.axis_index("tp")
    r = lax.rem(c, 2)
    y = lax.rem(c // 2, NY)
    x = c // (2 * NY)
    xpar = lax.rem(x, 2)
    ypar = lax.rem(y, 2)
    zpar = lax.rem(z, 2)

    def at(xx, yy, rr, zz):
        return ((xx * NY + yy) * 2 + rr, zz)

    def xo(d):
        return lax.rem(x + d + NX, NX)

    def yo(d):
        return lax.rem(y + d + NY, NY)

    def zo(d):
        return lax.rem(z + d + NZ, NZ)

    def copy(src, dst, ss, rs, dev):
        return pltpu.make_async_remote_copy(
            src_ref=src, dst_ref=dst, send_sem=ss, recv_sem=rs, device_id=dev, device_id_type=MESH)

    barrier = pltpu.get_barrier_semaphore()

    def greet(dev):
        pl.semaphore_signal(barrier, inc=1, device_id=dev, device_id_type=MESH)

    greet(at(x, y, 1 - r, z))
    for d in range(1, NX):
        greet(at(xo(d), y, r, z))
    for d in range(1, NY):
        greet(at(x, yo(d), r, z))
    for d in range(1, NZ):
        greet(at(x, y, r, zo(d)))
        greet(at(x, y, 1 - r, zo(d)))

    @pl.when(jnp.logical_and(r == 0, c > 0))
    def _():
        greet((c - 1, z))

    tokbuf[zpar * 2 + r] = tok_ref[...]
    ca = conv_ref[...]
    ca = jnp.concatenate([ca, ca], axis=0)
    taps_qk = ca[:, 0:128].T
    taps_v = ca[:, 32:WIDTH].T
    for o in range(4):
        cw[o, 0:32] = jnp.broadcast_to(taps_qk[0:32, o:o + 1], (32, 128))
        cw[o, 32:] = jnp.broadcast_to(taps_v[:, o:o + 1], (VW, 128))

    pl.semaphore_wait(barrier, NX + NY - 1 + 2 * (NZ - 1) + r * (1 - c // (2 * NX * NY - 1)))

    way_z = 2 * zpar - 1
    sends = []

    def guard(i, body):
        if i == 2:
            pl.when(r == 0)(body)
        else:
            body()

    def dist(i):
        return 5 - r - 2 * i

    zpair = z - way_z
    partner = at(x, y, 1 - r, z)
    own_tok = tokbuf.at[zpar * 2 + r]
    far_tok = tokbuf.at[(1 - zpar) * 2 + r]
    tok_near = copy(tok_ref, own_tok, tk_s.at[0], tk_r.at[0], partner)
    tok_pair = copy(tok_ref, own_tok, tk_s.at[1], tk_r.at[1], at(x, y, r, zpair))
    tok_relay = copy(far_tok, far_tok, tk_s.at[2], tk_r.at[2], partner)

    rhalf = pl.ds(pl.multiple_of(xpar * 80, 16), 80)
    xhalf = pl.ds(pl.multiple_of(ypar * 128, 128), 128)
    rpiece = proj_ref.at[rhalf, pl.ds(pl.multiple_of(y * 128, 128), 128)]
    xpiece = proj_ref.at[:, pl.ds(pl.multiple_of(1024 + x * 256 + ypar * 128, 128), 128)]
    zr, zx, xs, yb, ring, xb = {}, {}, {}, {}, {}, {}
    for i in range(3):
        d = dist(i)
        to = at(x, y, r, zo(d * (1 - 2 * lax.rem(z + d, 2))))
        zr[i] = copy(rpiece, wr.at[i, y, rhalf, :], zr_s.at[i], zr_r.at[i], to)
        zx[i] = copy(xpiece, wx.at[i, x, :, xhalf], zx_s.at[i], zx_r.at[i], to)
        ref = wr.at[i, y, rhalf, :]
        xs[i] = copy(ref, ref, xs_s.at[i], xs_r.at[i], at(x + 1 - 2 * xpar, y, r, z))
        ref = wx.at[i, x, :, xhalf]
        yb[i] = copy(ref, ref, yb_s.at[i], yb_r.at[i], at(x, y + 1 - 2 * ypar, r, z))
        for dx in range(1, NX):
            ref = wx.at[i, x]
            xb[i, dx] = copy(ref, ref, xb_s.at[i, dx - 1], xb_r.at[i, dx - 1], at(xo(dx), y, r, z))
        for s in range(1, 5):
            for way, sign in ((0, 1), (1, -1)):
                ref = wr.at[i, yo(-sign * (s - 1))]
                if s == 4:
                    ref = wr.at[i, yo(-sign * 3), pl.ds(80 * way, 80), :]
                ring[i, way, s] = copy(ref, ref, ya_s.at[i, way, s - 1], ya_r.at[i, way, s - 1], at(x, yo(sign), r, z))

    def z_start(i):
        zr[i].start()
        zx[i].start()

    def small(i):
        zr[i].wait_recv()
        xs[i].start()
        zx[i].wait_recv()
        yb[i].start()

    def first(i):
        xs[i].wait_recv()
        ring[i, 0, 1].start()
        ring[i, 1, 1].start()
        yb[i].wait_recv()
        for dx in range(1, NX):
            xb[i, dx].start()

    def step(i, s):
        for way in range(2):
            ring[i, way, s - 1].wait_recv()
            ring[i, way, s].start()

    def gathered(i):
        for dx in range(1, NX):
            xb[i, dx].wait_recv()
        for way in range(2):
            ring[i, way, 4].wait_recv()

    def project(i, block):
        acc = jnp.zeros((WIDTH, 4 * TILE), f32)
        for j in range(8):
            acc = acc + dot_nt(block(j), tokbuf[:, :, j * 256:(j + 1) * 256].reshape(4 * TILE, 256))
        for s in range(4):
            stage[i, s] = acc[:, s * TILE:(s + 1) * TILE].astype(bf16)

    def from_gather(i):
        def block(j):
            if j < 4:
                return jnp.concatenate([wr[i, 2 * j], wr[i, 2 * j + 1]], axis=1)
            return wx[i, j - 4]
        return block

    def from_own(j):
        return proj_ref[:, j * 256:(j + 1) * 256]

    tiles = {}
    for i in range(3):
        for s in range(4):
            source = 2 * (z // 2) + s // 2
            tiles[i, s] = copy(stage.at[i, s], xr.at[source + 1], at_s.at[i, s], at_r.at[source],
                               at(x, y, s % 2, zo(way_z * dist(i))))

    slots = range(3)
    for i in slots:
        guard(i, lambda i=i: z_start(i))
    tok_pair.start()
    tok_near.start()
    for i in slots:
        guard(i, lambda i=i: small(i))
    for i in slots:
        guard(i, lambda i=i: first(i))
    for i in slots:
        guard(i, lambda i=i: step(i, 2))
    tok_near.wait_recv()
    for i in slots:
        guard(i, lambda i=i: step(i, 3))
    tok_pair.wait_recv()
    tok_relay.start()
    for i in slots:
        guard(i, lambda i=i: step(i, 4))
    tok_relay.wait_recv()
    for i in range(2):
        gathered(i)
        project(i, from_gather(i))
        for s in range(4):
            tiles[i, s].start()

    @pl.when(r == 0)
    def _():
        gathered(2)
        project(2, from_gather(2))
        for s in range(4):
            tiles[2, s].start()

    @pl.when(r == 1)
    def _():
        project(2, from_own)
        for s in range(4):
            if s % 2 == 0:
                tiles[2, s].start()
            else:
                xr[2 * (z // 2) + s // 2 + 1] = stage[2, s]

    last = NZ - 1

    def tile_in(t):
        @pl.when(jnp.logical_or(r == 0, z // 2 != t // 2))
        def _():
            copy(stage.at[0, 0], xr.at[t + 1], at_s.at[0, 0], at_r.at[t], partner).wait_recv()

    def halo(dev):
        return copy(xr.at[NZ], xr.at[0], h_s, h_r, (dev, z))

    tile_in(last)

    @pl.when(c < 2 * NX * NY - 1)
    def _():
        halo(c + 1).start()

    for t in range(last):
        tile_in(t)

    @pl.when(c == 0)
    def _():
        xr[0] = jnp.zeros((WIDTH, TILE), bf16)

    @pl.when(c > 0)
    def _():
        halo(c - 1).wait_recv()

    lane = lax.broadcasted_iota(jnp.int32, (WIDTH, TILE), 1)
    quad = 1.0 / (2.0 ** 0.5 * FEAT ** 0.5)
    one_row = jnp.where(lax.broadcasted_iota(jnp.int32, (8, TILE), 0) == 0, 1.0, 0.0)

    def features(u, twice):
        parts = [u * u * quad]
        for d in range(1, 8):
            parts.append(u * pltpu.roll(u, FEAT - d, 0) * (quad * twice))
        parts.append((u * pltpu.roll(u, 8, 0) * (quad * twice))[:8])
        parts.append(u * FEAT ** -0.25)
        parts.append(one_row)
        return jnp.concatenate(parts, axis=0)

    @pl.loop(0, NZ)
    def _(t):
        before = xr[t].astype(f32)
        now = xr[t + 1].astype(f32)
        acc = cw[0] * now
        for o in range(1, 4):
            acc = acc + cw[o] * pltpu.roll(jnp.where(lane >= TILE - o, before, now), o, 1)
        vt[t] = acc[2 * FEAT:].astype(bf16)
        rows = pl.ds(pl.multiple_of(t * TILE, TILE), TILE)
        fq[rows, :] = features(acc[0:FEAT], 2.0).T.astype(bf16)
        fk[t] = features(acc[FEAT:2 * FEAT], 1.0).astype(bf16)

    per = BLOCK // TILE

    def lanes(ref, b, n):
        return jnp.concatenate([ref[b * per + t] for t in range(n)], axis=1)

    ones = jnp.ones((8, BLOCK), bf16)
    for b in range(2):
        keys = lanes(fk, b, per)
        st[b] = dot_nt(keys, lanes(vt, b, per))
        total = dot_nt(ones, keys)
        st[b, TOT:TOT + 1, :] = total[0:1, 0:128]
        st[b, TOT + 1:TOT + 2, 0:32] = total[0:1, 128:160]
    loc[...] = st[0] + st[1]

    mine = pl.ds(pl.multiple_of(r * HALF, 8), HALF)
    other = pl.ds(pl.multiple_of((1 - r) * HALF, 8), HALF)
    d1 = copy(loc.at[other, :], px, d1_s, d1_r, partner)
    d1.start()
    sends.append(d1)

    def within(b):
        for i in range(BLOCK // SUB):
            cols = (i + 1) * SUB
            keys = lanes(fk, b, cols // TILE)
            row = b * BLOCK + i * SUB
            w = jnp.dot(fq[row:row + SUB, :], keys, preferred_element_type=f32)
            causal = (lax.broadcasted_iota(jnp.int32, (SUB, cols), 0) + i * SUB
                      >= lax.broadcasted_iota(jnp.int32, (SUB, cols), 1))
            w = jnp.where(causal, w, 0.0)
            num[row:row + SUB, :] = dot_nt(w.astype(bf16), lanes(vt, b, cols // TILE))
            den[row:row + SUB, :] = jnp.broadcast_to(jnp.sum(w, axis=1, keepdims=True), (SUB, 128))

    d1.wait_recv()
    ch[...] = loc[mine, :] + px[...]
    sy = []
    for d in range(1, NY):
        cp = copy(ch, ybuf.at[d - 1], sy_s.at[d - 1], sy_r.at[d - 1], at(x, yo(d), r, z))
        cp.start()
        sy.append(cp)
    sends.extend(sy)
    within(0)
    within(1)
    total = ch[...]
    before = jnp.zeros((HALF, 128), f32)
    for d in range(1, NY):
        sy[d - 1].wait_recv()
        got = ybuf[d - 1]
        total = total + got
        before = before + jnp.where(y >= d, got, 0.0)
    tx[...] = total
    sx = []
    for d in range(1, NX):
        cp = copy(tx, xbuf.at[d - 1], sx_s.at[d - 1], sx_r.at[d - 1], at(xo(d), y, r, z))
        cp.start()
        sx.append(cp)
    sends.extend(sx)
    for d in range(1, NX):
        sx[d - 1].wait_recv()
        before = before + jnp.where(x >= d, xbuf[d - 1], 0.0)
    snd[...] = before + jnp.where(r == 0, loc[mine, :], 0.0)
    d2 = copy(snd, fin.at[mine, :], d2_s, d2_r, partner)
    d2.start()
    sends.append(d2)
    fin[mine, :] = before + jnp.where(r == 1, px[...], 0.0)
    d2.wait_recv()

    for b in range(2):
        state = fin[...] if b == 0 else fin[...] + st[0]
        high = state.astype(bf16)
        low = (state - high.astype(f32)).astype(bf16)
        row = jnp.concatenate([state[TOT:TOT + 1, :], state[TOT + 1:TOT + 2, 0:32]], axis=1)
        row_high = row.astype(bf16).astype(f32)
        which = lax.broadcasted_iota(jnp.int32, (16, PHI), 0)
        rows = jnp.where(which == 0, row_high, jnp.where(which == 1, row - row_high, 0.0)).astype(bf16)
        for i in range(BLOCK // SUB):
            at_rows = slice(b * BLOCK + i * SUB, b * BLOCK + (i + 1) * SUB)
            f = fq[at_rows, :]
            top = num[at_rows, :] + jnp.dot(f, high, preferred_element_type=f32)
            top = top + jnp.dot(f, low, preferred_element_type=f32)
            two = dot_nt(f, rows)
            bottom = den[at_rows, :] + (two[:, 0:1] + two[:, 1:2])
            out_ref[at_rows, :] = (top / bottom).astype(bf16)

    def left(i):
        zr[i].wait_send()
        zx[i].wait_send()
        xs[i].wait_send()
        yb[i].wait_send()
        for dx in range(1, NX):
            xb[i, dx].wait_send()
        for way in range(2):
            for s in range(1, 5):
                ring[i, way, s].wait_send()
        for s in range(1, 4, 2):
            tiles[i, s].wait_send()

    for i in range(3):
        guard(i, lambda i=i: left(i))
        for s in range(0, 4, 2):
            tiles[i, s].wait_send()
    for cp in (tok_near, tok_pair, tok_relay):
        cp.wait_send()
    for cp in sends:
        cp.wait_send()

    @pl.when(c < 2 * NX * NY - 1)
    def _():
        halo(c + 1).wait_send()


def per_device(tokens, projection, conv_weight):
    vmem = pltpu.VMEM
    dma = pltpu.SemaphoreType.DMA
    return pl.pallas_call(
        kernel,
        out_shape=jax.ShapeDtypeStruct((ROWS, VW), bf16),
        in_specs=[pl.BlockSpec(memory_space=vmem)] * 3,
        out_specs=pl.BlockSpec(memory_space=vmem),
        scratch_shapes=[
            vmem((4, TILE, D), bf16),
            vmem((3, NY, WIDTH, 128), bf16),
            vmem((3, NX, WIDTH, 256), bf16),
            vmem((3, 4, WIDTH, TILE), bf16),
            vmem((NZ + 1, WIDTH, TILE), bf16),
            vmem((4, WIDTH, TILE), f32),
            vmem((NZ, VW, TILE), bf16),
            vmem((ROWS, PHI), bf16),
            vmem((NZ, PHI, TILE), bf16),
            vmem((2, PHI, 128), f32),
            vmem((PHI, 128), f32),
            vmem((HALF, 128), f32),
            vmem((HALF, 128), f32),
            vmem((NY - 1, HALF, 128), f32),
            vmem((HALF, 128), f32),
            vmem((NX - 1, HALF, 128), f32),
            vmem((HALF, 128), f32),
            vmem((PHI, 128), f32),
            vmem((ROWS, 128), f32),
            vmem((ROWS, 128), f32),
            dma((3,)), dma((3,)),
            dma((3,)), dma((3,)),
            dma((3,)), dma((3,)),
            dma((3,)), dma((3,)),
            dma((3, 2, 4)), dma((3, 2, 4)),
            dma((3,)), dma((3,)),
            dma((3, NX - 1)), dma((3, NX - 1)),
            dma((3, 4)), dma((NZ,)),
            dma, dma,
            dma, dma,
            dma((NY - 1,)), dma((NY - 1,)),
            dma((NX - 1,)), dma((NX - 1,)),
            dma, dma,
        ],
        compiler_params=pltpu.CompilerParams(
            collective_id=0, has_side_effects=True, vmem_limit_bytes=48 * 2**20),
        name="fused",
    )(tokens, projection.T, conv_weight)


def solution(mesh):
    return jax.shard_map(
        per_device,
        mesh=mesh,
        in_specs=(P(("ctx", "tp"), None), P(None, "tp"), P(None, "tp")),
        out_specs=P("ctx", "tp"),
        check_vma=False,
    )
```

```python
import jax
import jax.numpy as jnp
from jax import lax
from jax.experimental import pallas as pl
from jax.experimental.pallas import tpu as pltpu
from jax.sharding import PartitionSpec as P

NX, NY, NZ = 4, 8, 12
D = 2048
FEAT = 16
VW = 128
WIDTH = 2 * FEAT + VW
TILE = 128
ROWS = TILE * NZ
PHI = 160
HALF = PHI // 2
PART = HALF // 2
TOT = 153
BLOCK = 768
SUB = 256
MESH = pl.DeviceIdType.MESH
bf16, f32 = jnp.bfloat16, jnp.float32


def dot_nt(a, b):
    return lax.dot_general(a, b, (((1,), (1,)), ((), ())), preferred_element_type=f32)


def kernel(tok_ref, proj_ref, conv_ref, out_ref,
           tokbuf, wr, wx, stage, xr, cw, vt, fq, fk, st, loc, px, ch, ybuf, tx, xbuf, pb, snd, fin, num, den,
           tk_s, tk_r, zr_s, zr_r, zx_s, zx_r, xs_s, xs_r, ya_s, ya_r, yb_s, yb_r, xb_s, xb_r, at_s, at_r, h_s, h_r,
           d1_s, d1_r, sy_s, sy_r, sx_s, sx_r, d2_s, d2_r):
    c = lax.axis_index("ctx")
    z = lax.axis_index("tp")
    r = lax.rem(c, 2)
    y = lax.rem(c // 2, NY)
    x = c // (2 * NY)
    xpar = lax.rem(x, 2)
    ypar = lax.rem(y, 2)
    zpar = lax.rem(z, 2)

    def at(xx, yy, rr, zz):
        return ((xx * NY + yy) * 2 + rr, zz)

    def xo(d):
        return lax.rem(x + d + NX, NX)

    def yo(d):
        return lax.rem(y + d + NY, NY)

    def zo(d):
        return lax.rem(z + d + NZ, NZ)

    def copy(src, dst, ss, rs, dev):
        return pltpu.make_async_remote_copy(
            src_ref=src, dst_ref=dst, send_sem=ss, recv_sem=rs, device_id=dev, device_id_type=MESH)

    barrier = pltpu.get_barrier_semaphore()

    def greet(dev):
        pl.semaphore_signal(barrier, inc=1, device_id=dev, device_id_type=MESH)

    greet(at(x, y, 1 - r, z))
    for d in range(1, NX):
        greet(at(xo(d), y, r, z))
    for d in range(1, NY):
        greet(at(x, yo(d), r, z))
    for d in range(1, NZ):
        greet(at(x, y, r, zo(d)))
        greet(at(x, y, 1 - r, zo(d)))

    @pl.when(jnp.logical_and(r == 0, c > 0))
    def _():
        greet((c - 1, z))

    tokbuf[zpar * 2 + r] = tok_ref[...]
    ca = conv_ref[...]
    ca = jnp.concatenate([ca, ca], axis=0)
    taps_qk = ca[:, 0:128].T
    taps_v = ca[:, 32:WIDTH].T
    for o in range(4):
        cw[o, 0:32] = jnp.broadcast_to(taps_qk[0:32, o:o + 1], (32, 128))
        cw[o, 32:] = jnp.broadcast_to(taps_v[:, o:o + 1], (VW, 128))

    pl.semaphore_wait(barrier, NX + NY - 1 + 2 * (NZ - 1) + r * (1 - c // (2 * NX * NY - 1)))

    way_z = 2 * zpar - 1
    sends = []

    def guard(i, body):
        if i == 2:
            pl.when(r == 0)(body)
        else:
            body()

    def dist(i):
        return 5 - r - 2 * i

    zpair = z - way_z
    partner = at(x, y, 1 - r, z)
    own_tok = tokbuf.at[zpar * 2 + r]
    far_tok = tokbuf.at[(1 - zpar) * 2 + r]
    tok_near = copy(tok_ref, own_tok, tk_s.at[0], tk_r.at[0], partner)
    tok_pair = copy(tok_ref, own_tok, tk_s.at[1], tk_r.at[1], at(x, y, r, zpair))
    tok_relay = copy(far_tok, far_tok, tk_s.at[2], tk_r.at[2], partner)

    rhalf = pl.ds(pl.multiple_of(xpar * 80, 16), 80)
    xhalf = pl.ds(pl.multiple_of(ypar * 128, 128), 128)
    rpiece = proj_ref.at[rhalf, pl.ds(pl.multiple_of(y * 128, 128), 128)]
    xpiece = proj_ref.at[:, pl.ds(pl.multiple_of(1024 + x * 256 + ypar * 128, 128), 128)]
    zr, zx, xs, yb, ring, xb = {}, {}, {}, {}, {}, {}
    for i in range(3):
        d = dist(i)
        to = at(x, y, r, zo(d * (1 - 2 * lax.rem(z + d, 2))))
        zr[i] = copy(rpiece, wr.at[i, y, rhalf, :], zr_s.at[i], zr_r.at[i], to)
        zx[i] = copy(xpiece, wx.at[i, x, :, xhalf], zx_s.at[i], zx_r.at[i], to)
        ref = wr.at[i, y, rhalf, :]
        xs[i] = copy(ref, ref, xs_s.at[i], xs_r.at[i], at(x + 1 - 2 * xpar, y, r, z))
        ref = wx.at[i, x, :, xhalf]
        yb[i] = copy(ref, ref, yb_s.at[i], yb_r.at[i], at(x, y + 1 - 2 * ypar, r, z))
        for dx in range(1, NX):
            ref = wx.at[i, x]
            xb[i, dx] = copy(ref, ref, xb_s.at[i, dx - 1], xb_r.at[i, dx - 1], at(xo(dx), y, r, z))
        for s in range(1, 5):
            for way, sign in ((0, 1), (1, -1)):
                ref = wr.at[i, yo(-sign * (s - 1))]
                if s == 4:
                    ref = wr.at[i, yo(-sign * 3), pl.ds(80 * way, 80), :]
                ring[i, way, s] = copy(ref, ref, ya_s.at[i, way, s - 1], ya_r.at[i, way, s - 1], at(x, yo(sign), r, z))

    def z_start(i):
        zr[i].start()
        zx[i].start()

    def small(i):
        zr[i].wait_recv()
        xs[i].start()
        zx[i].wait_recv()
        yb[i].start()

    def first(i):
        xs[i].wait_recv()
        ring[i, 0, 1].start()
        ring[i, 1, 1].start()
        yb[i].wait_recv()
        for dx in range(1, NX):
            xb[i, dx].start()

    def step(i, s):
        for way in range(2):
            ring[i, way, s - 1].wait_recv()
            ring[i, way, s].start()

    def gathered(i):
        for dx in range(1, NX):
            xb[i, dx].wait_recv()
        for way in range(2):
            ring[i, way, 4].wait_recv()

    def project(i, half, block):
        first_set = 2 * (zpar if half == 0 else 1 - zpar)
        acc = jnp.zeros((WIDTH, 2 * TILE), f32)
        for j in range(8):
            acc = acc + dot_nt(block(j), tokbuf[pl.ds(first_set, 2), :, j * 256:(j + 1) * 256].reshape(2 * TILE, 256))
        for q in range(2):
            stage[i, 2 * half + q] = acc[:, q * TILE:(q + 1) * TILE].astype(bf16)

    def from_gather(i):
        def block(j):
            if j < 4:
                return jnp.concatenate([wr[i, 2 * j], wr[i, 2 * j + 1]], axis=1)
            return wx[i, j - 4]
        return block

    def from_own(j):
        return proj_ref[:, j * 256:(j + 1) * 256]

    tiles = {}
    for i in range(3):
        for half, plane in ((0, z), (1, zpair)):
            for q in range(2):
                tiles[i, half, q] = copy(stage.at[i, 2 * half + q], xr.at[plane + 1], at_s.at[i, 2 * half + q],
                                         at_r.at[plane], at(x, y, q, zo(way_z * dist(i))))

    def work(i, half):
        project(i, half, from_gather(i))
        for q in range(2):
            tiles[i, half, q].start()

    def work_own(half, plane):
        project(2, half, from_own)
        tiles[2, half, 0].start()
        xr[plane + 1] = stage[2, 2 * half + 1]

    slots = range(3)
    for i in slots:
        guard(i, lambda i=i: z_start(i))
    tok_near.start()
    small(0)
    tok_pair.start()
    small(1)
    guard(2, lambda: small(2))
    for i in slots:
        guard(i, lambda i=i: first(i))
    for n in range(2, 5):
        for i in slots:
            guard(i, lambda i=i: step(i, n))
    tok_near.wait_recv()
    for i in range(2):
        gathered(i)
        work(i, 0)

    @pl.when(r == 0)
    def _():
        gathered(2)
        work(2, 0)

    tok_pair.wait_recv()
    tok_relay.start()

    @pl.when(r == 1)
    def _():
        work_own(0, z)

    tok_relay.wait_recv()
    for i in range(2):
        work(i, 1)

    @pl.when(r == 0)
    def _():
        work(2, 1)

    @pl.when(r == 1)
    def _():
        work_own(1, zpair)

    last = NZ - 1

    def tile_in(t):
        @pl.when(jnp.logical_or(r == 0, z // 2 != t // 2))
        def _():
            copy(stage.at[0, 0], xr.at[t + 1], at_s.at[0, 0], at_r.at[t], partner).wait_recv()

    def halo(dev):
        return copy(xr.at[NZ], xr.at[0], h_s, h_r, (dev, z))

    tile_in(last)

    @pl.when(c < 2 * NX * NY - 1)
    def _():
        halo(c + 1).start()

    for t in range(last):
        tile_in(t)

    lane = lax.broadcasted_iota(jnp.int32, (WIDTH, TILE), 1)
    quad = 1.0 / (2.0 ** 0.5 * FEAT ** 0.5)
    one_row = jnp.where(lax.broadcasted_iota(jnp.int32, (8, TILE), 0) == 0, 1.0, 0.0)

    def features(u, twice):
        parts = [u * u * quad]
        for d in range(1, 8):
            parts.append(u * pltpu.roll(u, FEAT - d, 0) * (quad * twice))
        parts.append((u * pltpu.roll(u, 8, 0) * (quad * twice))[:8])
        parts.append(u * FEAT ** -0.25)
        parts.append(one_row)
        return jnp.concatenate(parts, axis=0)

    def convolve(t):
        before = xr[t].astype(f32)
        now = xr[t + 1].astype(f32)
        acc = cw[0] * now
        for o in range(1, 4):
            acc = acc + cw[o] * pltpu.roll(jnp.where(lane >= TILE - o, before, now), o, 1)
        vt[t] = acc[2 * FEAT:].astype(bf16)
        rows = pl.ds(t * TILE if isinstance(t, int) else pl.multiple_of(t * TILE, TILE), TILE)
        fq[rows, :] = features(acc[0:FEAT], 2.0).T.astype(bf16)
        fk[t] = features(acc[FEAT:2 * FEAT], 1.0).astype(bf16)

    @pl.loop(1, NZ)
    def _(t):
        convolve(t)

    @pl.when(c == 0)
    def _():
        xr[0] = jnp.zeros((WIDTH, TILE), bf16)

    @pl.when(c > 0)
    def _():
        halo(c - 1).wait_recv()

    convolve(0)

    per = BLOCK // TILE

    def lanes(ref, b, n):
        return jnp.concatenate([ref[b * per + t] for t in range(n)], axis=1)

    ones = jnp.ones((8, BLOCK), bf16)
    for b in range(2):
        keys = lanes(fk, b, per)
        st[b] = dot_nt(keys, lanes(vt, b, per))
        total = dot_nt(ones, keys)
        st[b, TOT:TOT + 1, :] = total[0:1, 0:128]
        st[b, TOT + 1:TOT + 2, 0:32] = total[0:1, 128:160]
    loc[...] = st[0] + st[1]

    mine = pl.ds(pl.multiple_of(r * HALF, 8), HALF)
    other = pl.ds(pl.multiple_of((1 - r) * HALF, 8), HALF)
    d1 = copy(loc.at[other, :], px, d1_s, d1_r, partner)
    d1.start()
    sends.append(d1)

    def within(b):
        for i in range(BLOCK // SUB):
            cols = (i + 1) * SUB
            keys = lanes(fk, b, cols // TILE)
            row = b * BLOCK + i * SUB
            w = jnp.dot(fq[row:row + SUB, :], keys, preferred_element_type=f32)
            causal = (lax.broadcasted_iota(jnp.int32, (SUB, cols), 0) + i * SUB
                      >= lax.broadcasted_iota(jnp.int32, (SUB, cols), 1))
            w = jnp.where(causal, w, 0.0)
            num[row:row + SUB, :] = dot_nt(w.astype(bf16), lanes(vt, b, cols // TILE))
            den[row:row + SUB, :] = jnp.broadcast_to(jnp.sum(w, axis=1, keepdims=True), (SUB, 128))

    d1.wait_recv()
    chip = loc[mine, :] + px[...]
    ch[0] = chip[:PART]
    ch[1] = chip[PART:]

    def to_y(src, dst, ss, rs):
        out = []
        for d in range(1, NY):
            cp = copy(src(d), dst.at[d - 1], ss.at[d - 1], rs.at[d - 1], at(x, yo(d), r, z))
            cp.start()
            out.append(cp)
        sends.extend(out)
        return out

    def to_x(src, dst, ss, rs):
        out = []
        for d in range(1, NX):
            cp = copy(src, dst.at[d - 1], ss.at[d - 1], rs.at[d - 1], at(xo(d), y, r, z))
            cp.start()
            out.append(cp)
        sends.extend(out)
        return out

    x_second = to_x(ch.at[1], xbuf.at[1], sx_s.at[1], sx_r.at[1])
    y_first = to_y(lambda d: ch.at[0], ybuf.at[0], sy_s.at[0], sy_r.at[0])
    within(0)
    second = jnp.zeros((PART, 128), f32)
    for d in range(1, NX):
        x_second[d - 1].wait_recv()
        second = second + jnp.where(x >= d, xbuf[1, d - 1], 0.0)
    pb[0] = second
    pb[1] = second + ch[1]
    y_second = to_y(lambda d: pb.at[1 - (y + d) // NY], ybuf.at[1], sy_s.at[1], sy_r.at[1])
    within(1)
    total = ch[0]
    first_rows = jnp.zeros((PART, 128), f32)
    for d in range(1, NY):
        y_first[d - 1].wait_recv()
        got = ybuf[0, d - 1]
        total = total + got
        first_rows = first_rows + jnp.where(y >= d, got, 0.0)
    tx[...] = total
    x_first = to_x(tx, xbuf.at[0], sx_s.at[0], sx_r.at[0])
    for d in range(1, NY):
        y_second[d - 1].wait_recv()
        second = second + ybuf[1, d - 1]
    for d in range(1, NX):
        x_first[d - 1].wait_recv()
        first_rows = first_rows + jnp.where(x >= d, xbuf[0, d - 1], 0.0)
    before = jnp.concatenate([first_rows, second], axis=0)
    snd[...] = before + jnp.where(r == 0, loc[mine, :], 0.0)
    d2 = copy(snd, fin.at[mine, :], d2_s, d2_r, partner)
    d2.start()
    sends.append(d2)
    fin[mine, :] = before + jnp.where(r == 1, px[...], 0.0)
    d2.wait_recv()

    for b in range(2):
        state = fin[...] if b == 0 else fin[...] + st[0]
        high = state.astype(bf16)
        low = (state - high.astype(f32)).astype(bf16)
        row = jnp.concatenate([state[TOT:TOT + 1, :], state[TOT + 1:TOT + 2, 0:32]], axis=1)
        row_high = row.astype(bf16).astype(f32)
        which = lax.broadcasted_iota(jnp.int32, (16, PHI), 0)
        rows = jnp.where(which == 0, row_high, jnp.where(which == 1, row - row_high, 0.0)).astype(bf16)
        for i in range(BLOCK // SUB):
            at_rows = slice(b * BLOCK + i * SUB, b * BLOCK + (i + 1) * SUB)
            f = fq[at_rows, :]
            top = num[at_rows, :] + jnp.dot(f, high, preferred_element_type=f32)
            top = top + jnp.dot(f, low, preferred_element_type=f32)
            two = dot_nt(f, rows)
            bottom = den[at_rows, :] + (two[:, 0:1] + two[:, 1:2])
            out_ref[at_rows, :] = (top / bottom).astype(bf16)

    def left(i):
        zr[i].wait_send()
        zx[i].wait_send()
        xs[i].wait_send()
        yb[i].wait_send()
        for dx in range(1, NX):
            xb[i, dx].wait_send()
        for way in range(2):
            for s in range(1, 5):
                ring[i, way, s].wait_send()
        for half in range(2):
            tiles[i, half, 1].wait_send()

    for i in range(3):
        guard(i, lambda i=i: left(i))
        for half in range(2):
            tiles[i, half, 0].wait_send()
    for cp in (tok_near, tok_pair, tok_relay):
        cp.wait_send()
    for cp in sends:
        cp.wait_send()

    @pl.when(c < 2 * NX * NY - 1)
    def _():
        halo(c + 1).wait_send()


def per_device(tokens, projection, conv_weight):
    vmem = pltpu.VMEM
    dma = pltpu.SemaphoreType.DMA
    return pl.pallas_call(
        kernel,
        out_shape=jax.ShapeDtypeStruct((ROWS, VW), bf16),
        in_specs=[pl.BlockSpec(memory_space=vmem)] * 3,
        out_specs=pl.BlockSpec(memory_space=vmem),
        scratch_shapes=[
            vmem((4, TILE, D), bf16),
            vmem((3, NY, WIDTH, 128), bf16),
            vmem((3, NX, WIDTH, 256), bf16),
            vmem((3, 4, WIDTH, TILE), bf16),
            vmem((NZ + 1, WIDTH, TILE), bf16),
            vmem((4, WIDTH, TILE), f32),
            vmem((NZ, VW, TILE), bf16),
            vmem((ROWS, PHI), bf16),
            vmem((NZ, PHI, TILE), bf16),
            vmem((2, PHI, 128), f32),
            vmem((PHI, 128), f32),
            vmem((HALF, 128), f32),
            vmem((2, PART, 128), f32),
            vmem((2, NY - 1, PART, 128), f32),
            vmem((PART, 128), f32),
            vmem((2, NX - 1, PART, 128), f32),
            vmem((2, PART, 128), f32),
            vmem((HALF, 128), f32),
            vmem((PHI, 128), f32),
            vmem((ROWS, 128), f32),
            vmem((ROWS, 128), f32),
            dma((3,)), dma((3,)),
            dma((3,)), dma((3,)),
            dma((3,)), dma((3,)),
            dma((3,)), dma((3,)),
            dma((3, 2, 4)), dma((3, 2, 4)),
            dma((3,)), dma((3,)),
            dma((3, NX - 1)), dma((3, NX - 1)),
            dma((3, 4)), dma((NZ,)),
            dma, dma,
            dma, dma,
            dma((2, NY - 1)), dma((2, NY - 1)),
            dma((2, NX - 1)), dma((2, NX - 1)),
            dma, dma,
        ],
        compiler_params=pltpu.CompilerParams(
            collective_id=0, has_side_effects=True, vmem_limit_bytes=48 * 2**20),
        name="fused",
    )(tokens, projection.T, conv_weight)


def solution(mesh):
    return jax.shard_map(
        per_device,
        mesh=mesh,
        in_specs=(P(("ctx", "tp"), None), P(None, "tp"), P(None, "tp")),
        out_specs=P("ctx", "tp"),
        check_vma=False,
    )
```

```python
import jax
import jax.numpy as jnp
from jax import lax
from jax.experimental import pallas as pl
from jax.experimental.pallas import tpu as pltpu
from jax.sharding import PartitionSpec as P

NX, NY, NZ = 4, 8, 12
D = 2048
FEAT = 16
VW = 128
WIDTH = 2 * FEAT + VW
TILE = 128
ROWS = TILE * NZ
PHI = 160
HALF = PHI // 2
PART = HALF // 2
TOT = 153
BLOCK = 768
SUB = 256
MESH = pl.DeviceIdType.MESH
bf16, f32 = jnp.bfloat16, jnp.float32


def dot_nt(a, b):
    return lax.dot_general(a, b, (((1,), (1,)), ((), ())), preferred_element_type=f32)


def kernel(tok_ref, proj_ref, conv_ref, out_ref,
           own_w, taps, in_sem, tokbuf, wr, wx, stage, xr, cw, vt, fq, fk, st, loc, px, ch, ybuf, tx, xbuf, pb, snd, fin, num, den,
           tk_s, tk_r, zr_s, zr_r, zx_s, zx_r, xs_s, xs_r, ya_s, ya_r, yb_s, yb_r, xb_s, xb_r, at_s, at_r, h_s, h_r,
           d1_s, d1_r, sy_s, sy_r, sx_s, sx_r, d2_s, d2_r):
    c = lax.axis_index("ctx")
    z = lax.axis_index("tp")
    r = lax.rem(c, 2)
    y = lax.rem(c // 2, NY)
    x = c // (2 * NY)
    xpar = lax.rem(x, 2)
    ypar = lax.rem(y, 2)
    zpar = lax.rem(z, 2)

    def at(xx, yy, rr, zz):
        return ((xx * NY + yy) * 2 + rr, zz)

    def xo(d):
        return lax.rem(x + d + NX, NX)

    def yo(d):
        return lax.rem(y + d + NY, NY)

    def zo(d):
        return lax.rem(z + d + NZ, NZ)

    def copy(src, dst, ss, rs, dev):
        return pltpu.make_async_remote_copy(
            src_ref=src, dst_ref=dst, send_sem=ss, recv_sem=rs, device_id=dev, device_id_type=MESH)

    load_tok = pltpu.make_async_copy(tok_ref, tokbuf.at[zpar * 2 + r], in_sem.at[0])
    load_w = pltpu.make_async_copy(proj_ref, own_w, in_sem.at[1])
    load_taps = pltpu.make_async_copy(conv_ref, taps, in_sem.at[2])
    load_tok.start()
    load_w.start()
    load_taps.start()

    barrier = pltpu.get_barrier_semaphore()

    def greet(dev):
        pl.semaphore_signal(barrier, inc=1, device_id=dev, device_id_type=MESH)

    greet(at(x, y, 1 - r, z))
    for d in range(1, NX):
        greet(at(xo(d), y, r, z))
    for d in range(1, NY):
        greet(at(x, yo(d), r, z))
    for d in range(1, NZ):
        greet(at(x, y, r, zo(d)))
        greet(at(x, y, 1 - r, zo(d)))

    @pl.when(jnp.logical_and(r == 0, c > 0))
    def _():
        greet((c - 1, z))

    load_tok.wait()
    load_w.wait()
    load_taps.wait()
    ca = taps[...]
    ca = jnp.concatenate([ca, ca], axis=0)
    taps_qk = ca[:, 0:128].T
    taps_v = ca[:, 32:WIDTH].T
    for o in range(4):
        cw[o, 0:32] = jnp.broadcast_to(taps_qk[0:32, o:o + 1], (32, 128))
        cw[o, 32:] = jnp.broadcast_to(taps_v[:, o:o + 1], (VW, 128))

    pl.semaphore_wait(barrier, NX + NY - 1 + 2 * (NZ - 1) + r * (1 - c // (2 * NX * NY - 1)))

    way_z = 2 * zpar - 1
    sends = []

    def guard(i, body):
        if i == 2:
            pl.when(r == 0)(body)
        else:
            body()

    def dist(i):
        return 5 - r - 2 * i

    zpair = z - way_z
    partner = at(x, y, 1 - r, z)
    own_tok = tokbuf.at[zpar * 2 + r]
    far_tok = tokbuf.at[(1 - zpar) * 2 + r]
    tok_near = copy(own_tok, own_tok, tk_s.at[0], tk_r.at[0], partner)
    tok_pair = copy(own_tok, own_tok, tk_s.at[1], tk_r.at[1], at(x, y, r, zpair))
    tok_relay = copy(far_tok, far_tok, tk_s.at[2], tk_r.at[2], partner)

    rhalf = pl.ds(pl.multiple_of(xpar * 80, 16), 80)
    xhalf = pl.ds(pl.multiple_of(ypar * 128, 128), 128)
    rpiece = own_w.at[rhalf, pl.ds(pl.multiple_of(y * 128, 128), 128)]
    xpiece = own_w.at[:, pl.ds(pl.multiple_of(1024 + x * 256 + ypar * 128, 128), 128)]
    zr, zx, xs, yb, ring, xb = {}, {}, {}, {}, {}, {}
    for i in range(3):
        d = dist(i)
        to = at(x, y, r, zo(d * (1 - 2 * lax.rem(z + d, 2))))
        zr[i] = copy(rpiece, wr.at[i, y, rhalf, :], zr_s.at[i], zr_r.at[i], to)
        zx[i] = copy(xpiece, wx.at[i, x, :, xhalf], zx_s.at[i], zx_r.at[i], to)
        ref = wr.at[i, y, rhalf, :]
        xs[i] = copy(ref, ref, xs_s.at[i], xs_r.at[i], at(x + 1 - 2 * xpar, y, r, z))
        ref = wx.at[i, x, :, xhalf]
        yb[i] = copy(ref, ref, yb_s.at[i], yb_r.at[i], at(x, y + 1 - 2 * ypar, r, z))
        for dx in range(1, NX):
            ref = wx.at[i, x]
            xb[i, dx] = copy(ref, ref, xb_s.at[i, dx - 1], xb_r.at[i, dx - 1], at(xo(dx), y, r, z))
        for s in range(1, 5):
            for way, sign in ((0, 1), (1, -1)):
                ref = wr.at[i, yo(-sign * (s - 1))]
                if s == 4:
                    ref = wr.at[i, yo(-sign * 3), pl.ds(80 * way, 80), :]
                ring[i, way, s] = copy(ref, ref, ya_s.at[i, way, s - 1], ya_r.at[i, way, s - 1], at(x, yo(sign), r, z))

    def z_start(i):
        zr[i].start()
        zx[i].start()

    def small(i):
        zr[i].wait_recv()
        xs[i].start()
        zx[i].wait_recv()
        yb[i].start()

    def first(i):
        xs[i].wait_recv()
        for way in range(2):
            ring[i, way, 1].start()
        yb[i].wait_recv()
        for dx in range(1, NX):
            xb[i, dx].start()

    def step(i, s):
        for way in range(2):
            ring[i, way, s - 1].wait_recv()
            ring[i, way, s].start()

    def gathered(i):
        for dx in range(1, NX):
            xb[i, dx].wait_recv()
        for way in range(2):
            ring[i, way, 4].wait_recv()

    def project(i, half, block):
        first_set = 2 * (zpar if half == 0 else 1 - zpar)
        acc = jnp.zeros((WIDTH, 2 * TILE), f32)
        for j in range(8):
            acc = acc + dot_nt(block(j), tokbuf[pl.ds(first_set, 2), :, j * 256:(j + 1) * 256].reshape(2 * TILE, 256))
        for q in range(2):
            stage[i, 2 * half + q] = acc[:, q * TILE:(q + 1) * TILE].astype(bf16)

    def from_gather(i):
        def block(j):
            if j < 4:
                return jnp.concatenate([wr[i, 2 * j], wr[i, 2 * j + 1]], axis=1)
            return wx[i, j - 4]
        return block

    def from_own(j):
        return own_w[:, j * 256:(j + 1) * 256]

    tiles = {}
    for i in range(3):
        for half, plane in ((0, z), (1, zpair)):
            for q in range(2):
                tiles[i, half, q] = copy(stage.at[i, 2 * half + q], xr.at[plane + 1], at_s.at[i, 2 * half + q],
                                         at_r.at[plane], at(x, y, q, zo(way_z * dist(i))))

    def work(i, half):
        project(i, half, from_gather(i))
        for q in range(2):
            tiles[i, half, q].start()

    def work_own(half, plane):
        project(2, half, from_own)
        tiles[2, half, 0].start()
        xr[plane + 1] = stage[2, 2 * half + 1]

    def third(body):
        pl.when(r == 0)(body)

    z_start(0)
    tok_pair.start()
    tok_near.start()
    z_start(1)
    third(lambda: z_start(2))
    small(0)
    first(0)
    small(1)
    third(lambda: small(2))
    step(0, 2)
    first(1)
    step(0, 3)
    step(1, 2)
    third(lambda: first(2))
    step(0, 4)
    step(1, 3)
    third(lambda: step(2, 2))
    tok_near.wait_recv()
    gathered(0)
    work(0, 0)
    step(1, 4)
    third(lambda: step(2, 3))
    tok_pair.wait_recv()
    tok_relay.start()
    gathered(1)
    work(1, 0)
    third(lambda: step(2, 4))
    tok_relay.wait_recv()
    work(0, 1)
    work(1, 1)

    @pl.when(r == 0)
    def _():
        gathered(2)
        work(2, 0)
        work(2, 1)

    @pl.when(r == 1)
    def _():
        work_own(0, z)
        work_own(1, zpair)

    def tile_in(t):
        @pl.when(jnp.logical_or(r == 0, z // 2 != t // 2))
        def _():
            copy(stage.at[0, 0], xr.at[t + 1], at_s.at[0, 0], at_r.at[t], partner).wait_recv()

    def halo(dev):
        return copy(xr.at[NZ], xr.at[0], h_s, h_r, (dev, z))

    lane = lax.broadcasted_iota(jnp.int32, (WIDTH, TILE), 1)
    quad = 1.0 / (2.0 ** 0.5 * FEAT ** 0.5)
    one_row = jnp.where(lax.broadcasted_iota(jnp.int32, (8, TILE), 0) == 0, 1.0, 0.0)

    def features(u, twice):
        parts = [u * u * quad]
        for d in range(1, 8):
            parts.append(u * pltpu.roll(u, FEAT - d, 0) * (quad * twice))
        parts.append((u * pltpu.roll(u, 8, 0) * (quad * twice))[:8])
        parts.append(u * FEAT ** -0.25)
        parts.append(one_row)
        return jnp.concatenate(parts, axis=0)

    def convolve(t):
        before = xr[t].astype(f32)
        now = xr[t + 1].astype(f32)
        acc = cw[0] * now
        for o in range(1, 4):
            acc = acc + cw[o] * pltpu.roll(jnp.where(lane >= TILE - o, before, now), o, 1)
        vt[t] = acc[2 * FEAT:].astype(bf16)
        rows = pl.ds(t * TILE if isinstance(t, int) else pl.multiple_of(t * TILE, TILE), TILE)
        fq[rows, :] = features(acc[0:FEAT], 2.0).T.astype(bf16)
        fk[t] = features(acc[FEAT:2 * FEAT], 1.0).astype(bf16)

    a = 2 * (z // 2 + 2 + zpar)
    for pairs, ready in (((0, 1), (1, 2, 3)), ((-1, 2), (-1, 0, 4, 5)), ((-2, 3), (-4, -3, -2, 6, 7))):
        here = [lax.rem(a + 2 * p + q + NZ, NZ) for p in pairs for q in range(2)]
        for t in here:
            tile_in(t)

        @pl.when(jnp.logical_and(c < 2 * NX * NY - 1, jnp.logical_or(here[1] == NZ - 1, here[3] == NZ - 1)))
        def _():
            halo(c + 1).start()

        for n in ready:
            t = lax.rem(a + n + NZ, NZ)

            @pl.when(t != 0)
            def _():
                convolve(t)

    @pl.when(c == 0)
    def _():
        xr[0] = jnp.zeros((WIDTH, TILE), bf16)

    @pl.when(c > 0)
    def _():
        halo(c - 1).wait_recv()

    convolve(0)

    per = BLOCK // TILE

    def lanes(ref, b, n):
        return jnp.concatenate([ref[b * per + t] for t in range(n)], axis=1)

    ones = jnp.ones((8, BLOCK), bf16)
    for b in range(2):
        keys = lanes(fk, b, per)
        st[b] = dot_nt(keys, lanes(vt, b, per))
        total = dot_nt(ones, keys)
        st[b, TOT:TOT + 1, :] = total[0:1, 0:128]
        st[b, TOT + 1:TOT + 2, 0:32] = total[0:1, 128:160]
    loc[...] = st[0] + st[1]

    mine = pl.ds(pl.multiple_of(r * HALF, 8), HALF)
    other = pl.ds(pl.multiple_of((1 - r) * HALF, 8), HALF)
    d1 = copy(loc.at[other, :], px, d1_s, d1_r, partner)
    d1.start()
    sends.append(d1)

    def within(b):
        for i in range(BLOCK // SUB):
            cols = (i + 1) * SUB
            keys = lanes(fk, b, cols // TILE)
            row = b * BLOCK + i * SUB
            w = jnp.dot(fq[row:row + SUB, :], keys, preferred_element_type=f32)
            causal = (lax.broadcasted_iota(jnp.int32, (SUB, cols), 0) + i * SUB
                      >= lax.broadcasted_iota(jnp.int32, (SUB, cols), 1))
            w = jnp.where(causal, w, 0.0)
            num[row:row + SUB, :] = dot_nt(w.astype(bf16), lanes(vt, b, cols // TILE))
            den[row:row + SUB, :] = jnp.broadcast_to(jnp.sum(w, axis=1, keepdims=True), (SUB, 128))

    d1.wait_recv()
    chip = loc[mine, :] + px[...]
    ch[0] = chip[:PART]
    ch[1] = chip[PART:]

    def to_y(src, dst, ss, rs):
        out = []
        for d in range(1, NY):
            cp = copy(src(d), dst.at[d - 1], ss.at[d - 1], rs.at[d - 1], at(x, yo(d), r, z))
            cp.start()
            out.append(cp)
        sends.extend(out)
        return out

    def to_x(src, dst, ss, rs):
        out = []
        for d in range(1, NX):
            cp = copy(src, dst.at[d - 1], ss.at[d - 1], rs.at[d - 1], at(xo(d), y, r, z))
            cp.start()
            out.append(cp)
        sends.extend(out)
        return out

    x_second = to_x(ch.at[1], xbuf.at[1], sx_s.at[1], sx_r.at[1])
    y_first = to_y(lambda d: ch.at[0], ybuf.at[0], sy_s.at[0], sy_r.at[0])
    within(0)
    second = jnp.zeros((PART, 128), f32)
    for d in range(1, NX):
        x_second[d - 1].wait_recv()
        second = second + jnp.where(x >= d, xbuf[1, d - 1], 0.0)
    pb[0] = second
    pb[1] = second + ch[1]
    y_second = to_y(lambda d: pb.at[1 - (y + d) // NY], ybuf.at[1], sy_s.at[1], sy_r.at[1])
    within(1)
    total = ch[0]
    first_rows = jnp.zeros((PART, 128), f32)
    for d in range(1, NY):
        y_first[d - 1].wait_recv()
        got = ybuf[0, d - 1]
        total = total + got
        first_rows = first_rows + jnp.where(y >= d, got, 0.0)
    tx[...] = total
    x_first = to_x(tx, xbuf.at[0], sx_s.at[0], sx_r.at[0])
    for d in range(1, NY):
        y_second[d - 1].wait_recv()
        second = second + ybuf[1, d - 1]
    for d in range(1, NX):
        x_first[d - 1].wait_recv()
        first_rows = first_rows + jnp.where(x >= d, xbuf[0, d - 1], 0.0)
    before = jnp.concatenate([first_rows, second], axis=0)
    snd[...] = before + jnp.where(r == 0, loc[mine, :], 0.0)
    d2 = copy(snd, fin.at[mine, :], d2_s, d2_r, partner)
    d2.start()
    sends.append(d2)
    fin[mine, :] = before + jnp.where(r == 1, px[...], 0.0)
    d2.wait_recv()

    for b in range(2):
        state = fin[...] if b == 0 else fin[...] + st[0]
        high = state.astype(bf16)
        low = (state - high.astype(f32)).astype(bf16)
        row = jnp.concatenate([state[TOT:TOT + 1, :], state[TOT + 1:TOT + 2, 0:32]], axis=1)
        row_high = row.astype(bf16).astype(f32)
        which = lax.broadcasted_iota(jnp.int32, (16, PHI), 0)
        rows = jnp.where(which == 0, row_high, jnp.where(which == 1, row - row_high, 0.0)).astype(bf16)
        for i in range(BLOCK // SUB):
            at_rows = slice(b * BLOCK + i * SUB, b * BLOCK + (i + 1) * SUB)
            f = fq[at_rows, :]
            top = num[at_rows, :] + jnp.dot(f, high, preferred_element_type=f32)
            top = top + jnp.dot(f, low, preferred_element_type=f32)
            two = dot_nt(f, rows)
            bottom = den[at_rows, :] + (two[:, 0:1] + two[:, 1:2])
            out_ref[at_rows, :] = (top / bottom).astype(bf16)

    def left(i):
        zr[i].wait_send()
        zx[i].wait_send()
        xs[i].wait_send()
        yb[i].wait_send()
        for dx in range(1, NX):
            xb[i, dx].wait_send()
        for way in range(2):
            for s in range(1, 5):
                ring[i, way, s].wait_send()
        for half in range(2):
            tiles[i, half, 1].wait_send()

    for i in range(3):
        guard(i, lambda i=i: left(i))
        for half in range(2):
            tiles[i, half, 0].wait_send()
    for cp in (tok_near, tok_pair, tok_relay):
        cp.wait_send()
    for cp in sends:
        cp.wait_send()

    @pl.when(c < 2 * NX * NY - 1)
    def _():
        halo(c + 1).wait_send()


def per_device(tokens, projection, conv_weight):
    vmem = pltpu.VMEM
    dma = pltpu.SemaphoreType.DMA
    return pl.pallas_call(
        kernel,
        out_shape=jax.ShapeDtypeStruct((ROWS, VW), bf16),
        in_specs=[pl.BlockSpec(memory_space=pl.ANY)] * 3,
        out_specs=pl.BlockSpec(memory_space=vmem),
        scratch_shapes=[
            vmem((WIDTH, D), bf16),
            vmem((4, WIDTH), f32),
            dma((3,)),
            vmem((4, TILE, D), bf16),
            vmem((3, NY, WIDTH, 128), bf16),
            vmem((3, NX, WIDTH, 256), bf16),
            vmem((3, 4, WIDTH, TILE), bf16),
            vmem((NZ + 1, WIDTH, TILE), bf16),
            vmem((4, WIDTH, TILE), f32),
            vmem((NZ, VW, TILE), bf16),
            vmem((ROWS, PHI), bf16),
            vmem((NZ, PHI, TILE), bf16),
            vmem((2, PHI, 128), f32),
            vmem((PHI, 128), f32),
            vmem((HALF, 128), f32),
            vmem((2, PART, 128), f32),
            vmem((2, NY - 1, PART, 128), f32),
            vmem((PART, 128), f32),
            vmem((2, NX - 1, PART, 128), f32),
            vmem((2, PART, 128), f32),
            vmem((HALF, 128), f32),
            vmem((PHI, 128), f32),
            vmem((ROWS, 128), f32),
            vmem((ROWS, 128), f32),
            dma((3,)), dma((3,)),
            dma((3,)), dma((3,)),
            dma((3,)), dma((3,)),
            dma((3,)), dma((3,)),
            dma((3, 2, 4)), dma((3, 2, 4)),
            dma((3,)), dma((3,)),
            dma((3, NX - 1)), dma((3, NX - 1)),
            dma((3, 4)), dma((NZ,)),
            dma, dma,
            dma, dma,
            dma((2, NY - 1)), dma((2, NY - 1)),
            dma((2, NX - 1)), dma((2, NX - 1)),
            dma, dma,
        ],
        compiler_params=pltpu.CompilerParams(
            collective_id=0, has_side_effects=True, vmem_limit_bytes=60 * 2**20),
        name="fused",
    )(tokens, projection.T, conv_weight)


def solution(mesh):
    return jax.shard_map(
        per_device,
        mesh=mesh,
        in_specs=(P(("ctx", "tp"), None), P(None, "tp"), P(None, "tp")),
        out_specs=P("ctx", "tp"),
        check_vma=False,
    )
```

```python
import jax
import jax.numpy as jnp
from jax import lax
from jax.experimental import pallas as pl
from jax.experimental.pallas import tpu as pltpu
from jax.sharding import PartitionSpec as P

NX, NY, NZ = 4, 8, 12
D = 2048
FEAT = 16
KY = D // 4
KX = (D - KY) // NX
VW = 128
WIDTH = 2 * FEAT + VW
TILE = 128
ROWS = TILE * NZ
PHI = 160
HALF = PHI // 2
PART = HALF // 2
TOT = 153
BLOCK = 768
SUB = 256
MESH = pl.DeviceIdType.MESH
bf16, f32 = jnp.bfloat16, jnp.float32


def dot_nt(a, b):
    return lax.dot_general(a, b, (((1,), (1,)), ((), ())), preferred_element_type=f32)


def kernel(tok_ref, proj_ref, conv_ref, out_ref,
           own_w, taps, in_sem, tokbuf, wr, wx, stage, xr, cw, vt, fq, fk, st, loc, px, ch, ybuf, tx, xbuf, pb, snd, fin, num, den,
           tk_s, tk_r, zr_s, zr_r, zx_s, zx_r, ya_s, ya_r, yb_s, yb_r, xb_s, xb_r, at_s, at_r, h_s, h_r,
           d1_s, d1_r, sy_s, sy_r, sx_s, sx_r, d2_s, d2_r):
    c = lax.axis_index("ctx")
    z = lax.axis_index("tp")
    r = lax.rem(c, 2)
    y = lax.rem(c // 2, NY)
    x = c // (2 * NY)
    ypar = lax.rem(y, 2)
    zpar = lax.rem(z, 2)

    def at(xx, yy, rr, zz):
        return ((xx * NY + yy) * 2 + rr, zz)

    def xo(d):
        return lax.rem(x + d + NX, NX)

    def yo(d):
        return lax.rem(y + d + NY, NY)

    def zo(d):
        return lax.rem(z + d + NZ, NZ)

    def copy(src, dst, ss, rs, dev):
        return pltpu.make_async_remote_copy(
            src_ref=src, dst_ref=dst, send_sem=ss, recv_sem=rs, device_id=dev, device_id_type=MESH)

    load_tok = pltpu.make_async_copy(tok_ref, tokbuf.at[zpar * 2 + r], in_sem.at[0])
    load_w = pltpu.make_async_copy(proj_ref, own_w, in_sem.at[1])
    load_taps = pltpu.make_async_copy(conv_ref, taps, in_sem.at[2])
    load_tok.start()
    load_w.start()
    load_taps.start()

    barrier = pltpu.get_barrier_semaphore()

    def greet(dev):
        pl.semaphore_signal(barrier, inc=1, device_id=dev, device_id_type=MESH)

    greet(at(x, y, 1 - r, z))
    for d in range(1, NX):
        greet(at(xo(d), y, r, z))
    for d in range(1, NY):
        greet(at(x, yo(d), r, z))
    for d in range(1, NZ):
        greet(at(x, y, r, zo(d)))
        greet(at(x, y, 1 - r, zo(d)))

    @pl.when(jnp.logical_and(r == 0, c > 0))
    def _():
        greet((c - 1, z))

    load_tok.wait()
    load_w.wait()
    load_taps.wait()
    ca = taps[...]
    ca = jnp.concatenate([ca, ca], axis=0)
    taps_qk = ca[:, 0:128].T
    taps_v = ca[:, 32:WIDTH].T
    for o in range(4):
        cw[o, 0:32] = jnp.broadcast_to(taps_qk[0:32, o:o + 1], (32, 128))
        cw[o, 32:] = jnp.broadcast_to(taps_v[:, o:o + 1], (VW, 128))

    pl.semaphore_wait(barrier, NX + NY - 1 + 2 * (NZ - 1) + r * (1 - c // (2 * NX * NY - 1)))

    way_z = 2 * zpar - 1
    sends = []

    def guard(i, body):
        if i == 2:
            pl.when(r == 0)(body)
        else:
            body()

    def dist(i):
        return 5 - r - 2 * i

    zpair = z - way_z
    partner = at(x, y, 1 - r, z)
    own_tok = tokbuf.at[zpar * 2 + r]
    far_tok = tokbuf.at[(1 - zpar) * 2 + r]
    tok_near = copy(own_tok, own_tok, tk_s.at[0], tk_r.at[0], partner)
    tok_pair = copy(own_tok, own_tok, tk_s.at[1], tk_r.at[1], at(x, y, r, zpair))
    tok_relay = copy(far_tok, far_tok, tk_s.at[2], tk_r.at[2], partner)

    rows = pl.ds(pl.multiple_of(ypar * 80, 16), 80)
    xlanes = pl.ds(pl.multiple_of(KY + x * KX, 128), KX)
    zr, zx, yb, ya, xb = {}, {}, {}, {}, {}
    for i in range(3):
        d = dist(i)
        to = at(x, y, r, zo(d * (1 - 2 * lax.rem(z + d, 2))))
        block = wr.at[i, y // 2, rows, :]
        zr[i] = copy(own_w.at[rows, pl.ds(pl.multiple_of(y // 2 * 128, 128), 128)], block, zr_s.at[i], zr_r.at[i], to)
        for dy in range(1, NY):
            ya[i, dy] = copy(block, block, ya_s.at[i, dy - 1], ya_r.at[i, dy - 1], at(x, yo(dy), r, z))
        block = wx.at[i, x, rows, :]
        zx[i] = copy(own_w.at[rows, xlanes], block, zx_s.at[i], zx_r.at[i], to)
        yb[i] = copy(block, block, yb_s.at[i], yb_r.at[i], at(x, y + 1 - 2 * ypar, r, z))
        block = wx.at[i, x]
        for dx in range(1, NX):
            xb[i, dx] = copy(block, block, xb_s.at[i, dx - 1], xb_r.at[i, dx - 1], at(xo(dx), y, r, z))

    def z_start(i):
        zr[i].start()
        zx[i].start()

    def small(i):
        zx[i].wait_recv()
        yb[i].start()
        zr[i].wait_recv()
        for dy in (4, 3, 5, 2, 6, 1, 7):
            ya[i, dy].start()

    def large(i):
        yb[i].wait_recv()
        for dx in (2, 1, 3):
            xb[i, dx].start()

    def gathered(i):
        for dx in range(1, NX):
            xb[i, dx].wait_recv()
        for dy in range(1, NY):
            ya[i, dy].wait_recv()

    def project(i, half, block):
        first_set = 2 * (zpar if half == 0 else 1 - zpar)
        acc = jnp.zeros((WIDTH, 2 * TILE), f32)
        for j in range(6):
            k = slice(j * 256, (j + 1) * 256) if j < 2 else slice(KY + (j - 2) * KX, KY + (j - 1) * KX)
            acc = acc + dot_nt(block(j, k), tokbuf[pl.ds(first_set, 2), :, k].reshape(2 * TILE, k.stop - k.start))
        for q in range(2):
            stage[i, 2 * half + q] = acc[:, q * TILE:(q + 1) * TILE].astype(bf16)

    def from_gather(i):
        def block(j, k):
            if j < 2:
                return jnp.concatenate([wr[i, 2 * j], wr[i, 2 * j + 1]], axis=1)
            return wx[i, j - 2]
        return block

    def from_own(j, k):
        return own_w[:, k]

    tiles = {}
    for i in range(3):
        for half, plane in ((0, z), (1, zpair)):
            for q in range(2):
                tiles[i, half, q] = copy(stage.at[i, 2 * half + q], xr.at[plane + 1], at_s.at[i, 2 * half + q],
                                         at_r.at[plane], at(x, y, q, zo(way_z * dist(i))))

    def work(i, half):
        project(i, half, from_gather(i))
        for q in range(2):
            tiles[i, half, q].start()

    def work_own(half, plane):
        project(2, half, from_own)
        tiles[2, half, 0].start()
        xr[plane + 1] = stage[2, 2 * half + 1]

    def third(body):
        pl.when(r == 0)(body)

    z_start(0)
    z_start(1)
    third(lambda: z_start(2))
    tok_near.start()
    small(0)
    tok_pair.start()
    large(0)
    small(1)
    third(lambda: small(2))
    large(1)
    third(lambda: large(2))
    tok_near.wait_recv()
    gathered(0)
    work(0, 0)
    tok_pair.wait_recv()
    tok_relay.start()
    tok_relay.wait_recv()
    work(0, 1)
    gathered(1)
    work(1, 0)
    work(1, 1)

    @pl.when(r == 0)
    def _():
        gathered(2)
        work(2, 0)
        work(2, 1)

    @pl.when(r == 1)
    def _():
        work_own(0, z)
        work_own(1, zpair)

    def tile_in(t):
        @pl.when(jnp.logical_or(r == 0, z // 2 != t // 2))
        def _():
            copy(stage.at[0, 0], xr.at[t + 1], at_s.at[0, 0], at_r.at[t], partner).wait_recv()

    def halo(dev):
        return copy(xr.at[NZ], xr.at[0], h_s, h_r, (dev, z))

    lane = lax.broadcasted_iota(jnp.int32, (WIDTH, TILE), 1)
    quad = 1.0 / (2.0 ** 0.5 * FEAT ** 0.5)
    one_row = jnp.where(lax.broadcasted_iota(jnp.int32, (8, TILE), 0) == 0, 1.0, 0.0)

    def features(u, twice):
        parts = [u * u * quad]
        for d in range(1, 8):
            parts.append(u * pltpu.roll(u, FEAT - d, 0) * (quad * twice))
        parts.append((u * pltpu.roll(u, 8, 0) * (quad * twice))[:8])
        parts.append(u * FEAT ** -0.25)
        parts.append(one_row)
        return jnp.concatenate(parts, axis=0)

    def convolve(t):
        before = xr[t].astype(f32)
        now = xr[t + 1].astype(f32)
        acc = cw[0] * now
        for o in range(1, 4):
            acc = acc + cw[o] * pltpu.roll(jnp.where(lane >= TILE - o, before, now), o, 1)
        vt[t] = acc[2 * FEAT:].astype(bf16)
        rows = pl.ds(t * TILE if isinstance(t, int) else pl.multiple_of(t * TILE, TILE), TILE)
        fq[rows, :] = features(acc[0:FEAT], 2.0).T.astype(bf16)
        fk[t] = features(acc[FEAT:2 * FEAT], 1.0).astype(bf16)

    a = 2 * (z // 2 + 2 + zpar)
    for pairs, ready in (((0, 1), (1, 2, 3)), ((-1, 2), (-1, 0, 4, 5)), ((-2, 3), (-4, -3, -2, 6, 7))):
        here = [lax.rem(a + 2 * p + q + NZ, NZ) for p in pairs for q in range(2)]
        for t in here:
            tile_in(t)

        @pl.when(jnp.logical_and(c < 2 * NX * NY - 1, jnp.logical_or(here[1] == NZ - 1, here[3] == NZ - 1)))
        def _():
            halo(c + 1).start()

        for n in ready:
            t = lax.rem(a + n + NZ, NZ)

            @pl.when(t != 0)
            def _():
                convolve(t)

    @pl.when(c == 0)
    def _():
        xr[0] = jnp.zeros((WIDTH, TILE), bf16)

    @pl.when(c > 0)
    def _():
        halo(c - 1).wait_recv()

    convolve(0)

    per = BLOCK // TILE

    def lanes(ref, b, n):
        return jnp.concatenate([ref[b * per + t] for t in range(n)], axis=1)

    ones = jnp.ones((8, BLOCK), bf16)
    for b in range(2):
        keys = lanes(fk, b, per)
        st[b] = dot_nt(keys, lanes(vt, b, per))
        total = dot_nt(ones, keys)
        st[b, TOT:TOT + 1, :] = total[0:1, 0:128]
        st[b, TOT + 1:TOT + 2, 0:32] = total[0:1, 128:160]
    loc[...] = st[0] + st[1]

    mine = pl.ds(pl.multiple_of(r * HALF, 8), HALF)
    other = pl.ds(pl.multiple_of((1 - r) * HALF, 8), HALF)
    d1 = copy(loc.at[other, :], px, d1_s, d1_r, partner)
    d1.start()
    sends.append(d1)

    def within(b):
        for i in range(BLOCK // SUB):
            cols = (i + 1) * SUB
            keys = lanes(fk, b, cols // TILE)
            row = b * BLOCK + i * SUB
            w = jnp.dot(fq[row:row + SUB, :], keys, preferred_element_type=f32)
            causal = (lax.broadcasted_iota(jnp.int32, (SUB, cols), 0) + i * SUB
                      >= lax.broadcasted_iota(jnp.int32, (SUB, cols), 1))
            w = jnp.where(causal, w, 0.0)
            num[row:row + SUB, :] = dot_nt(w.astype(bf16), lanes(vt, b, cols // TILE))
            den[row:row + SUB, :] = jnp.broadcast_to(jnp.sum(w, axis=1, keepdims=True), (SUB, 128))

    d1.wait_recv()
    chip = loc[mine, :] + px[...]
    ch[0] = chip[:PART]
    ch[1] = chip[PART:]

    def to_y(src, dst, ss, rs):
        out = []
        for d in range(1, NY):
            cp = copy(src(d), dst.at[d - 1], ss.at[d - 1], rs.at[d - 1], at(x, yo(d), r, z))
            cp.start()
            out.append(cp)
        sends.extend(out)
        return out

    def to_x(src, dst, ss, rs):
        out = []
        for d in range(1, NX):
            cp = copy(src, dst.at[d - 1], ss.at[d - 1], rs.at[d - 1], at(xo(d), y, r, z))
            cp.start()
            out.append(cp)
        sends.extend(out)
        return out

    x_second = to_x(ch.at[1], xbuf.at[1], sx_s.at[1], sx_r.at[1])
    y_first = to_y(lambda d: ch.at[0], ybuf.at[0], sy_s.at[0], sy_r.at[0])
    within(0)
    second = jnp.zeros((PART, 128), f32)
    for d in range(1, NX):
        x_second[d - 1].wait_recv()
        second = second + jnp.where(x >= d, xbuf[1, d - 1], 0.0)
    pb[0] = second
    pb[1] = second + ch[1]
    y_second = to_y(lambda d: pb.at[1 - (y + d) // NY], ybuf.at[1], sy_s.at[1], sy_r.at[1])
    within(1)
    total = ch[0]
    first_rows = jnp.zeros((PART, 128), f32)
    for d in range(1, NY):
        y_first[d - 1].wait_recv()
        got = ybuf[0, d - 1]
        total = total + got
        first_rows = first_rows + jnp.where(y >= d, got, 0.0)
    tx[...] = total
    x_first = to_x(tx, xbuf.at[0], sx_s.at[0], sx_r.at[0])
    for d in range(1, NY):
        y_second[d - 1].wait_recv()
        second = second + ybuf[1, d - 1]
    for d in range(1, NX):
        x_first[d - 1].wait_recv()
        first_rows = first_rows + jnp.where(x >= d, xbuf[0, d - 1], 0.0)
    before = jnp.concatenate([first_rows, second], axis=0)
    snd[...] = before + jnp.where(r == 0, loc[mine, :], 0.0)
    d2 = copy(snd, fin.at[mine, :], d2_s, d2_r, partner)
    d2.start()
    sends.append(d2)
    fin[mine, :] = before + jnp.where(r == 1, px[...], 0.0)
    d2.wait_recv()

    for b in range(2):
        state = fin[...] if b == 0 else fin[...] + st[0]
        high = state.astype(bf16)
        low = (state - high.astype(f32)).astype(bf16)
        row = jnp.concatenate([state[TOT:TOT + 1, :], state[TOT + 1:TOT + 2, 0:32]], axis=1)
        row_high = row.astype(bf16).astype(f32)
        which = lax.broadcasted_iota(jnp.int32, (16, PHI), 0)
        rows = jnp.where(which == 0, row_high, jnp.where(which == 1, row - row_high, 0.0)).astype(bf16)
        for i in range(BLOCK // SUB):
            at_rows = slice(b * BLOCK + i * SUB, b * BLOCK + (i + 1) * SUB)
            f = fq[at_rows, :]
            top = num[at_rows, :] + jnp.dot(f, high, preferred_element_type=f32)
            top = top + jnp.dot(f, low, preferred_element_type=f32)
            two = dot_nt(f, rows)
            bottom = den[at_rows, :] + (two[:, 0:1] + two[:, 1:2])
            out_ref[at_rows, :] = (top / bottom).astype(bf16)

    def left(i):
        zr[i].wait_send()
        zx[i].wait_send()
        yb[i].wait_send()
        for dx in range(1, NX):
            xb[i, dx].wait_send()
        for dy in range(1, NY):
            ya[i, dy].wait_send()
        for half in range(2):
            tiles[i, half, 1].wait_send()

    for i in range(3):
        guard(i, lambda i=i: left(i))
        for half in range(2):
            tiles[i, half, 0].wait_send()
    for cp in (tok_near, tok_pair, tok_relay):
        cp.wait_send()
    for cp in sends:
        cp.wait_send()

    @pl.when(c < 2 * NX * NY - 1)
    def _():
        halo(c + 1).wait_send()


def per_device(tokens, projection, conv_weight):
    vmem = pltpu.VMEM
    dma = pltpu.SemaphoreType.DMA
    return pl.pallas_call(
        kernel,
        out_shape=jax.ShapeDtypeStruct((ROWS, VW), bf16),
        in_specs=[pl.BlockSpec(memory_space=pl.ANY)] * 3,
        out_specs=pl.BlockSpec(memory_space=vmem),
        scratch_shapes=[
            vmem((WIDTH, D), bf16),
            vmem((4, WIDTH), f32),
            dma((3,)),
            vmem((4, TILE, D), bf16),
            vmem((3, KY // 128, WIDTH, 128), bf16),
            vmem((3, NX, WIDTH, KX), bf16),
            vmem((3, 4, WIDTH, TILE), bf16),
            vmem((NZ + 1, WIDTH, TILE), bf16),
            vmem((4, WIDTH, TILE), f32),
            vmem((NZ, VW, TILE), bf16),
            vmem((ROWS, PHI), bf16),
            vmem((NZ, PHI, TILE), bf16),
            vmem((2, PHI, 128), f32),
            vmem((PHI, 128), f32),
            vmem((HALF, 128), f32),
            vmem((2, PART, 128), f32),
            vmem((2, NY - 1, PART, 128), f32),
            vmem((PART, 128), f32),
            vmem((2, NX - 1, PART, 128), f32),
            vmem((2, PART, 128), f32),
            vmem((HALF, 128), f32),
            vmem((PHI, 128), f32),
            vmem((ROWS, 128), f32),
            vmem((ROWS, 128), f32),
            dma((3,)), dma((3,)),
            dma((3,)), dma((3,)),
            dma((3,)), dma((3,)),
            dma((3, NY - 1)), dma((3, NY - 1)),
            dma((3,)), dma((3,)),
            dma((3, NX - 1)), dma((3, NX - 1)),
            dma((3, 4)), dma((NZ,)),
            dma, dma,
            dma, dma,
            dma((2, NY - 1)), dma((2, NY - 1)),
            dma((2, NX - 1)), dma((2, NX - 1)),
            dma, dma,
        ],
        compiler_params=pltpu.CompilerParams(
            collective_id=0, has_side_effects=True, vmem_limit_bytes=107 * 2**19),
        name="fused",
    )(tokens, projection.T, conv_weight)


def solution(mesh):
    return jax.shard_map(
        per_device,
        mesh=mesh,
        in_specs=(P(("ctx", "tp"), None), P(None, "tp"), P(None, "tp")),
        out_specs=P("ctx", "tp"),
        check_vma=False,
    )
```

```python
import jax
import jax.numpy as jnp
from jax import lax
from jax.experimental import pallas as pl
from jax.experimental.pallas import tpu as pltpu
from jax.sharding import PartitionSpec as P

NX, NY, NZ = 4, 8, 12
D = 2048
FEAT = 16
KY = D // 4
KX = (D - KY) // NX
VW = 128
WIDTH = 2 * FEAT + VW
TILE = 128
ROWS = TILE * NZ
PHI = 160
HALF = PHI // 2
PART = HALF // 2
TOT = 153
BLOCK = 768
SUB = 256
MESH = pl.DeviceIdType.MESH
bf16, f32 = jnp.bfloat16, jnp.float32


def dot_nt(a, b):
    return lax.dot_general(a, b, (((1,), (1,)), ((), ())), preferred_element_type=f32)


def kernel(tok_ref, proj_ref, conv_ref, out_ref,
           own_w, taps, in_sem, tokbuf, wr, wx, stage, xr, cw, vt, fq, fk, st, loc, px, ch, ybuf, tx, xbuf, pb, snd, fin, num, den,
           tk_s, tk_r, zr_s, zr_r, zx_s, zx_r, ya_s, ya_r, yb_s, yb_r, xb_s, xb_r, at_s, at_r, h_s, h_r,
           d1_s, d1_r, sy_s, sy_r, sx_s, sx_r, d2_s, d2_r):
    c = lax.axis_index("ctx")
    z = lax.axis_index("tp")
    r = lax.rem(c, 2)
    y = lax.rem(c // 2, NY)
    x = c // (2 * NY)
    ypar = lax.rem(y, 2)
    zpar = lax.rem(z, 2)

    def at(xx, yy, rr, zz):
        return ((xx * NY + yy) * 2 + rr, zz)

    def xo(d):
        return lax.rem(x + d + NX, NX)

    def yo(d):
        return lax.rem(y + d + NY, NY)

    def zo(d):
        return lax.rem(z + d + NZ, NZ)

    def copy(src, dst, ss, rs, dev):
        return pltpu.make_async_remote_copy(
            src_ref=src, dst_ref=dst, send_sem=ss, recv_sem=rs, device_id=dev, device_id_type=MESH)

    load_tok = pltpu.make_async_copy(tok_ref, tokbuf.at[zpar * 2 + r], in_sem.at[0])
    load_w = pltpu.make_async_copy(proj_ref, own_w, in_sem.at[1])
    load_taps = pltpu.make_async_copy(conv_ref, taps, in_sem.at[2])
    load_tok.start()
    load_w.start()
    load_taps.start()

    barrier = pltpu.get_barrier_semaphore()

    def greet(dev):
        pl.semaphore_signal(barrier, inc=1, device_id=dev, device_id_type=MESH)

    greet(at(x, y, 1 - r, z))
    for d in range(1, NX):
        greet(at(xo(d), y, r, z))
    for d in range(1, NY):
        greet(at(x, yo(d), r, z))
    for d in range(1, NZ):
        greet(at(x, y, r, zo(d)))
        greet(at(x, y, 1 - r, zo(d)))

    @pl.when(jnp.logical_and(r == 0, c > 0))
    def _():
        greet((c - 1, z))

    pl.semaphore_wait(barrier, NX + NY - 1 + 2 * (NZ - 1) + r * (1 - c // (2 * NX * NY - 1)))

    way_z = 2 * zpar - 1
    sends = []

    def guard(i, body):
        if i == 2:
            pl.when(r == 0)(body)
        else:
            body()

    def dist(i):
        return 5 - r - 2 * i

    zpair = z - way_z
    partner = at(x, y, 1 - r, z)
    own_tok = tokbuf.at[zpar * 2 + r]
    far_tok = tokbuf.at[(1 - zpar) * 2 + r]
    tok_near = copy(own_tok, own_tok, tk_s.at[0], tk_r.at[0], partner)
    tok_pair = copy(own_tok, own_tok, tk_s.at[1], tk_r.at[1], at(x, y, r, zpair))
    tok_relay = copy(far_tok, far_tok, tk_s.at[2], tk_r.at[2], partner)

    rows = pl.ds(pl.multiple_of(ypar * 80, 16), 80)
    xlanes = pl.ds(pl.multiple_of(KY + x * KX, 128), KX)
    zr, zx, yb, ya, xb = {}, {}, {}, {}, {}
    for i in range(3):
        d = dist(i)
        to = at(x, y, r, zo(d * (1 - 2 * lax.rem(z + d, 2))))
        block = wr.at[i, y // 2, rows, :]
        zr[i] = copy(own_w.at[rows, pl.ds(pl.multiple_of(y // 2 * 128, 128), 128)], block, zr_s.at[i], zr_r.at[i], to)
        for dy in range(1, NY):
            ya[i, dy] = copy(block, block, ya_s.at[i, dy - 1], ya_r.at[i, dy - 1], at(x, yo(dy), r, z))
        block = wx.at[i, x, rows, :]
        zx[i] = copy(own_w.at[rows, xlanes], block, zx_s.at[i], zx_r.at[i], to)
        yb[i] = copy(block, block, yb_s.at[i], yb_r.at[i], at(x, y + 1 - 2 * ypar, r, z))
        block = wx.at[i, x]
        for dx in range(1, NX):
            xb[i, dx] = copy(block, block, xb_s.at[i, dx - 1], xb_r.at[i, dx - 1], at(xo(dx), y, r, z))

    def z_start(i):
        zx[i].start()
        zr[i].start()

    def small(i):
        zx[i].wait_recv()
        yb[i].start()
        zr[i].wait_recv()
        for dy in (4, 3, 5, 2, 6, 1, 7):
            ya[i, dy].start()

    def large(i):
        yb[i].wait_recv()
        for dx in (2, 1, 3):
            xb[i, dx].start()

    def gathered(i):
        for dx in range(1, NX):
            xb[i, dx].wait_recv()
        for dy in range(1, NY):
            ya[i, dy].wait_recv()

    def project(i, half, block):
        first_set = 2 * (zpar if half == 0 else 1 - zpar)
        acc = jnp.zeros((WIDTH, 2 * TILE), f32)
        for j in range(6):
            k = slice(j * 256, (j + 1) * 256) if j < 2 else slice(KY + (j - 2) * KX, KY + (j - 1) * KX)
            acc = acc + dot_nt(block(j, k), tokbuf[pl.ds(first_set, 2), :, k].reshape(2 * TILE, k.stop - k.start))
        for q in range(2):
            stage[i, 2 * half + q] = acc[:, q * TILE:(q + 1) * TILE].astype(bf16)

    def from_gather(i):
        def block(j, k):
            if j < 2:
                return jnp.concatenate([wr[i, 2 * j], wr[i, 2 * j + 1]], axis=1)
            return wx[i, j - 2]
        return block

    def from_own(j, k):
        return own_w[:, k]

    tiles = {}
    for i in range(3):
        for half, plane in ((0, z), (1, zpair)):
            for q in range(2):
                tiles[i, half, q] = copy(stage.at[i, 2 * half + q], xr.at[plane + 1], at_s.at[i, 2 * half + q],
                                         at_r.at[plane], at(x, y, q, zo(way_z * dist(i))))

    def work(i, half):
        project(i, half, from_gather(i))
        for q in range(2):
            tiles[i, half, q].start()

    def work_own(half, plane):
        project(2, half, from_own)
        tiles[2, half, 0].start()
        xr[plane + 1] = stage[2, 2 * half + 1]

    def third(body):
        pl.when(r == 0)(body)

    load_w.wait()
    z_start(0)
    z_start(1)
    third(lambda: z_start(2))
    load_tok.wait()
    tok_near.start()
    load_taps.wait()
    ca = taps[...]
    ca = jnp.concatenate([ca, ca], axis=0)
    taps_qk = ca[:, 0:128].T
    taps_v = ca[:, 32:WIDTH].T
    for o in range(4):
        cw[o, 0:32] = jnp.broadcast_to(taps_qk[0:32, o:o + 1], (32, 128))
        cw[o, 32:] = jnp.broadcast_to(taps_v[:, o:o + 1], (VW, 128))
    small(0)
    tok_pair.start()
    large(0)
    small(1)
    third(lambda: small(2))
    large(1)
    third(lambda: large(2))
    tok_near.wait_recv()
    gathered(0)
    work(0, 0)
    tok_pair.wait_recv()
    tok_relay.start()
    tok_relay.wait_recv()
    work(0, 1)
    gathered(1)
    work(1, 0)
    work(1, 1)

    @pl.when(r == 0)
    def _():
        gathered(2)
        work(2, 0)
        work(2, 1)

    @pl.when(r == 1)
    def _():
        work_own(0, z)
        work_own(1, zpair)

    def tile_in(t):
        @pl.when(jnp.logical_or(r == 0, z // 2 != t // 2))
        def _():
            copy(stage.at[0, 0], xr.at[t + 1], at_s.at[0, 0], at_r.at[t], partner).wait_recv()

    def halo(dev):
        return copy(xr.at[NZ], xr.at[0], h_s, h_r, (dev, z))

    lane = lax.broadcasted_iota(jnp.int32, (WIDTH, TILE), 1)
    quad = 1.0 / (2.0 ** 0.5 * FEAT ** 0.5)
    one_row = jnp.where(lax.broadcasted_iota(jnp.int32, (8, TILE), 0) == 0, 1.0, 0.0)

    def features(u, twice):
        parts = [u * u * quad]
        for d in range(1, 8):
            parts.append(u * pltpu.roll(u, FEAT - d, 0) * (quad * twice))
        parts.append((u * pltpu.roll(u, 8, 0) * (quad * twice))[:8])
        parts.append(u * FEAT ** -0.25)
        parts.append(one_row)
        return jnp.concatenate(parts, axis=0)

    def convolve(t):
        before = xr[t].astype(f32)
        now = xr[t + 1].astype(f32)
        acc = cw[0] * now
        for o in range(1, 4):
            acc = acc + cw[o] * pltpu.roll(jnp.where(lane >= TILE - o, before, now), o, 1)
        vt[t] = acc[2 * FEAT:].astype(bf16)
        rows = pl.ds(t * TILE if isinstance(t, int) else pl.multiple_of(t * TILE, TILE), TILE)
        fq[rows, :] = features(acc[0:FEAT], 2.0).T.astype(bf16)
        fk[t] = features(acc[FEAT:2 * FEAT], 1.0).astype(bf16)

    a = 2 * (z // 2 + 2 + zpar)
    for pairs, ready in (((0, 1), (1, 2, 3)), ((-1, 2), (-1, 0, 4, 5)), ((-2, 3), (-4, -3, -2, 6, 7))):
        here = [lax.rem(a + 2 * p + q + NZ, NZ) for p in pairs for q in range(2)]
        for t in here:
            tile_in(t)

        @pl.when(jnp.logical_and(c < 2 * NX * NY - 1, jnp.logical_or(here[1] == NZ - 1, here[3] == NZ - 1)))
        def _():
            halo(c + 1).start()

        for n in ready:
            t = lax.rem(a + n + NZ, NZ)

            @pl.when(t != 0)
            def _():
                convolve(t)

    @pl.when(c == 0)
    def _():
        xr[0] = jnp.zeros((WIDTH, TILE), bf16)

    @pl.when(c > 0)
    def _():
        halo(c - 1).wait_recv()

    convolve(0)

    per = BLOCK // TILE

    def lanes(ref, b, n):
        return jnp.concatenate([ref[b * per + t] for t in range(n)], axis=1)

    ones = jnp.ones((8, BLOCK), bf16)
    for b in range(2):
        keys = lanes(fk, b, per)
        st[b] = dot_nt(keys, lanes(vt, b, per))
        total = dot_nt(ones, keys)
        st[b, TOT:TOT + 1, :] = total[0:1, 0:128]
        st[b, TOT + 1:TOT + 2, 0:32] = total[0:1, 128:160]
    loc[...] = st[0] + st[1]

    mine = pl.ds(pl.multiple_of(r * HALF, 8), HALF)
    other = pl.ds(pl.multiple_of((1 - r) * HALF, 8), HALF)
    d1 = copy(loc.at[other, :], px, d1_s, d1_r, partner)
    d1.start()
    sends.append(d1)

    def within(b):
        for i in range(BLOCK // SUB):
            cols = (i + 1) * SUB
            keys = lanes(fk, b, cols // TILE)
            row = b * BLOCK + i * SUB
            w = jnp.dot(fq[row:row + SUB, :], keys, preferred_element_type=f32)
            causal = (lax.broadcasted_iota(jnp.int32, (SUB, cols), 0) + i * SUB
                      >= lax.broadcasted_iota(jnp.int32, (SUB, cols), 1))
            w = jnp.where(causal, w, 0.0)
            num[row:row + SUB, :] = dot_nt(w.astype(bf16), lanes(vt, b, cols // TILE))
            den[row:row + SUB, :] = jnp.broadcast_to(jnp.sum(w, axis=1, keepdims=True), (SUB, 128))

    d1.wait_recv()
    chip = loc[mine, :] + px[...]
    ch[0] = chip[:PART]
    ch[1] = chip[PART:]

    def to_y(src, dst, ss, rs):
        out = []
        for d in range(1, NY):
            out.append(copy(src(d), dst.at[d - 1], ss.at[d - 1], rs.at[d - 1], at(x, yo(d), r, z)))
        for d in (4, 3, 5, 2, 6, 1, 7):
            out[d - 1].start()
        sends.extend(out)
        return out

    def to_x(src, dst, ss, rs):
        out = []
        for d in range(1, NX):
            cp = copy(src, dst.at[d - 1], ss.at[d - 1], rs.at[d - 1], at(xo(d), y, r, z))
            cp.start()
            out.append(cp)
        sends.extend(out)
        return out

    x_second = to_x(ch.at[1], xbuf.at[1], sx_s.at[1], sx_r.at[1])
    y_first = to_y(lambda d: ch.at[0], ybuf.at[0], sy_s.at[0], sy_r.at[0])
    within(0)
    second = jnp.zeros((PART, 128), f32)
    for d in range(1, NX):
        x_second[d - 1].wait_recv()
        second = second + jnp.where(x >= d, xbuf[1, d - 1], 0.0)
    pb[0] = second
    pb[1] = second + ch[1]
    y_second = to_y(lambda d: pb.at[1 - (y + d) // NY], ybuf.at[1], sy_s.at[1], sy_r.at[1])
    within(1)
    total = ch[0]
    first_rows = jnp.zeros((PART, 128), f32)
    for d in range(1, NY):
        y_first[d - 1].wait_recv()
        got = ybuf[0, d - 1]
        total = total + got
        first_rows = first_rows + jnp.where(y >= d, got, 0.0)
    tx[...] = total
    x_first = to_x(tx, xbuf.at[0], sx_s.at[0], sx_r.at[0])
    for d in range(1, NY):
        y_second[d - 1].wait_recv()
        second = second + ybuf[1, d - 1]
    for d in range(1, NX):
        x_first[d - 1].wait_recv()
        first_rows = first_rows + jnp.where(x >= d, xbuf[0, d - 1], 0.0)
    before = jnp.concatenate([first_rows, second], axis=0)
    snd[...] = before + jnp.where(r == 0, loc[mine, :], 0.0)
    d2 = copy(snd, fin.at[mine, :], d2_s, d2_r, partner)
    d2.start()
    sends.append(d2)
    fin[mine, :] = before + jnp.where(r == 1, px[...], 0.0)
    d2.wait_recv()

    for b in range(2):
        state = fin[...] if b == 0 else fin[...] + st[0]
        high = state.astype(bf16)
        low = (state - high.astype(f32)).astype(bf16)
        row = jnp.concatenate([state[TOT:TOT + 1, :], state[TOT + 1:TOT + 2, 0:32]], axis=1)
        row_high = row.astype(bf16).astype(f32)
        which = lax.broadcasted_iota(jnp.int32, (16, PHI), 0)
        rows = jnp.where(which == 0, row_high, jnp.where(which == 1, row - row_high, 0.0)).astype(bf16)
        for i in range(BLOCK // SUB):
            at_rows = slice(b * BLOCK + i * SUB, b * BLOCK + (i + 1) * SUB)
            f = fq[at_rows, :]
            top = num[at_rows, :] + jnp.dot(f, high, preferred_element_type=f32)
            top = top + jnp.dot(f, low, preferred_element_type=f32)
            two = dot_nt(f, rows)
            bottom = den[at_rows, :] + (two[:, 0:1] + two[:, 1:2])
            out_ref[at_rows, :] = (top / bottom).astype(bf16)

    def left(i):
        zr[i].wait_send()
        zx[i].wait_send()
        yb[i].wait_send()
        for dx in range(1, NX):
            xb[i, dx].wait_send()
        for dy in range(1, NY):
            ya[i, dy].wait_send()
        for half in range(2):
            tiles[i, half, 1].wait_send()

    for i in range(3):
        guard(i, lambda i=i: left(i))
        for half in range(2):
            tiles[i, half, 0].wait_send()
    for cp in (tok_near, tok_pair, tok_relay):
        cp.wait_send()
    for cp in sends:
        cp.wait_send()

    @pl.when(c < 2 * NX * NY - 1)
    def _():
        halo(c + 1).wait_send()


def per_device(tokens, projection, conv_weight):
    vmem = pltpu.VMEM
    dma = pltpu.SemaphoreType.DMA
    return pl.pallas_call(
        kernel,
        out_shape=jax.ShapeDtypeStruct((ROWS, VW), bf16),
        in_specs=[pl.BlockSpec(memory_space=pl.ANY)] * 3,
        out_specs=pl.BlockSpec(memory_space=vmem),
        scratch_shapes=[
            vmem((WIDTH, D), bf16),
            vmem((4, WIDTH), f32),
            dma((3,)),
            vmem((4, TILE, D), bf16),
            vmem((3, KY // 128, WIDTH, 128), bf16),
            vmem((3, NX, WIDTH, KX), bf16),
            vmem((3, 4, WIDTH, TILE), bf16),
            vmem((NZ + 1, WIDTH, TILE), bf16),
            vmem((4, WIDTH, TILE), f32),
            vmem((NZ, VW, TILE), bf16),
            vmem((ROWS, PHI), bf16),
            vmem((NZ, PHI, TILE), bf16),
            vmem((2, PHI, 128), f32),
            vmem((PHI, 128), f32),
            vmem((HALF, 128), f32),
            vmem((2, PART, 128), f32),
            vmem((2, NY - 1, PART, 128), f32),
            vmem((PART, 128), f32),
            vmem((2, NX - 1, PART, 128), f32),
            vmem((2, PART, 128), f32),
            vmem((HALF, 128), f32),
            vmem((PHI, 128), f32),
            vmem((ROWS, 128), f32),
            vmem((ROWS, 128), f32),
            dma((3,)), dma((3,)),
            dma((3,)), dma((3,)),
            dma((3,)), dma((3,)),
            dma((3, NY - 1)), dma((3, NY - 1)),
            dma((3,)), dma((3,)),
            dma((3, NX - 1)), dma((3, NX - 1)),
            dma((3, 4)), dma((NZ,)),
            dma, dma,
            dma, dma,
            dma((2, NY - 1)), dma((2, NY - 1)),
            dma((2, NX - 1)), dma((2, NX - 1)),
            dma, dma,
        ],
        compiler_params=pltpu.CompilerParams(
            collective_id=0, has_side_effects=True, vmem_limit_bytes=107 * 2**19),
        name="fused",
    )(tokens, projection.T, conv_weight)


def solution(mesh):
    return jax.shard_map(
        per_device,
        mesh=mesh,
        in_specs=(P(("ctx", "tp"), None), P(None, "tp"), P(None, "tp")),
        out_specs=P("ctx", "tp"),
        check_vma=False,
    )
```

```python
import jax
import jax.numpy as jnp
from jax import lax
from jax.experimental import pallas as pl
from jax.experimental.pallas import tpu as pltpu
from jax.sharding import PartitionSpec as P

NX, NY, NZ = 4, 8, 12
D = 2048
FEAT = 16
KY = D // 4
KX = (D - KY) // NX
VW = 128
WIDTH = 2 * FEAT + VW
TILE = 128
ROWS = TILE * NZ
PHI = 160
HALF = PHI // 2
PART = HALF // 2
TOT = 153
BLOCK = 768
SUB = 256
MESH = pl.DeviceIdType.MESH
bf16, f32 = jnp.bfloat16, jnp.float32


def dot_nt(a, b):
    return lax.dot_general(a, b, (((1,), (1,)), ((), ())), preferred_element_type=f32)


def kernel(tok_ref, proj_ref, conv_ref, out_ref,
           own_w, taps, in_sem, tokbuf, wr, wx, stage, xr, cw, vt, fq, fk, st, loc, px, ch, ybuf, tx, xbuf, pb, snd, fin, num, den,
           tk_s, tk_r, zr_s, zr_r, zx_s, zx_r, ya_s, ya_r, yb_s, yb_r, xb_s, xb_r, at_s, at_r, h_s, h_r,
           d1_s, d1_r, sy_s, sy_r, sx_s, sx_r, d2_s, d2_r):
    c = lax.axis_index("ctx")
    z = lax.axis_index("tp")
    r = lax.rem(c, 2)
    y = lax.rem(c // 2, NY)
    x = c // (2 * NY)
    ypar = lax.rem(y, 2)
    zpar = lax.rem(z, 2)

    def at(xx, yy, rr, zz):
        return ((xx * NY + yy) * 2 + rr, zz)

    def xo(d):
        return lax.rem(x + d + NX, NX)

    def yo(d):
        return lax.rem(y + d + NY, NY)

    def zo(d):
        return lax.rem(z + d + NZ, NZ)

    def copy(src, dst, ss, rs, dev):
        return pltpu.make_async_remote_copy(
            src_ref=src, dst_ref=dst, send_sem=ss, recv_sem=rs, device_id=dev, device_id_type=MESH)

    load_tok = pltpu.make_async_copy(tok_ref, tokbuf.at[zpar * 2 + r], in_sem.at[0])
    load_w = pltpu.make_async_copy(proj_ref, own_w, in_sem.at[1])
    load_taps = pltpu.make_async_copy(conv_ref, taps, in_sem.at[2])
    load_tok.start()
    load_w.start()
    load_taps.start()

    barrier = pltpu.get_barrier_semaphore()

    def greet(dev):
        pl.semaphore_signal(barrier, inc=1, device_id=dev, device_id_type=MESH)

    greet(at(x, y, 1 - r, z))
    for d in range(1, NX):
        greet(at(xo(d), y, r, z))
    for d in range(1, NY):
        greet(at(x, yo(d), r, z))
    for d in range(1, NZ):
        greet(at(x, y, r, zo(d)))
        greet(at(x, y, 1 - r, zo(d)))

    @pl.when(jnp.logical_and(r == 0, c > 0))
    def _():
        greet((c - 1, z))

    load_tok.wait()
    load_w.wait()
    load_taps.wait()
    ca = taps[...]
    ca = jnp.concatenate([ca, ca], axis=0)
    taps_qk = ca[:, 0:128].T
    taps_v = ca[:, 32:WIDTH].T
    for o in range(4):
        cw[o, 0:32] = jnp.broadcast_to(taps_qk[0:32, o:o + 1], (32, 128))
        cw[o, 32:] = jnp.broadcast_to(taps_v[:, o:o + 1], (VW, 128))

    pl.semaphore_wait(barrier, NX + NY - 1 + 2 * (NZ - 1) + r * (1 - c // (2 * NX * NY - 1)))

    way_z = 2 * zpar - 1
    sends = []

    def guard(i, body):
        if i == 2:
            pl.when(r == 0)(body)
        else:
            body()

    def dist(i):
        return 5 - r - 2 * i

    zpair = z - way_z
    partner = at(x, y, 1 - r, z)
    own_tok = tokbuf.at[zpar * 2 + r]
    far_tok = tokbuf.at[(1 - zpar) * 2 + r]
    tok_near = copy(own_tok, own_tok, tk_s.at[0], tk_r.at[0], partner)
    tok_pair = copy(own_tok, own_tok, tk_s.at[1], tk_r.at[1], at(x, y, r, zpair))
    tok_relay = copy(far_tok, far_tok, tk_s.at[2], tk_r.at[2], partner)

    rows = pl.ds(pl.multiple_of(ypar * 80, 16), 80)
    xlanes = pl.ds(pl.multiple_of(KY + x * KX, 128), KX)
    zr, zx, yb, ya, xb = {}, {}, {}, {}, {}
    for i in range(3):
        d = dist(i)
        to = at(x, y, r, zo(d * (1 - 2 * lax.rem(z + d, 2))))
        block = wr.at[i, y // 2, rows, :]
        zr[i] = copy(own_w.at[rows, pl.ds(pl.multiple_of(y // 2 * 128, 128), 128)], block, zr_s.at[i], zr_r.at[i], to)
        for dy in range(1, NY):
            ya[i, dy] = copy(block, block, ya_s.at[i, dy - 1], ya_r.at[i, dy - 1], at(x, yo(dy), r, z))
        block = wx.at[i, x, rows, :]
        zx[i] = copy(own_w.at[rows, xlanes], block, zx_s.at[i], zx_r.at[i], to)
        yb[i] = copy(block, block, yb_s.at[i], yb_r.at[i], at(x, y + 1 - 2 * ypar, r, z))
        block = wx.at[i, x]
        for dx in range(1, NX):
            xb[i, dx] = copy(block, block, xb_s.at[i, dx - 1], xb_r.at[i, dx - 1], at(xo(dx), y, r, z))

    def z_start(i):
        zr[i].start()
        zx[i].start()

    def small(i):
        zx[i].wait_recv()
        yb[i].start()
        zr[i].wait_recv()
        for dy in (4, 3, 5, 2, 6, 1, 7):
            ya[i, dy].start()

    def large(i):
        yb[i].wait_recv()
        for dx in (2, 1, 3):
            xb[i, dx].start()

    def gathered(i):
        for dx in range(1, NX):
            xb[i, dx].wait_recv()
        for dy in range(1, NY):
            ya[i, dy].wait_recv()

    def project(i, half, block):
        first_set = 2 * (zpar if half == 0 else 1 - zpar)
        acc = jnp.zeros((WIDTH, 2 * TILE), f32)
        for j in range(6):
            k = slice(j * 256, (j + 1) * 256) if j < 2 else slice(KY + (j - 2) * KX, KY + (j - 1) * KX)
            acc = acc + dot_nt(block(j, k), tokbuf[pl.ds(first_set, 2), :, k].reshape(2 * TILE, k.stop - k.start))
        for q in range(2):
            stage[i, 2 * half + q] = acc[:, q * TILE:(q + 1) * TILE].astype(bf16)

    def from_gather(i):
        def block(j, k):
            if j < 2:
                return jnp.concatenate([wr[i, 2 * j], wr[i, 2 * j + 1]], axis=1)
            return wx[i, j - 2]
        return block

    def from_own(j, k):
        return own_w[:, k]

    tiles = {}
    for i in range(3):
        for half, plane in ((0, z), (1, zpair)):
            for q in range(2):
                tiles[i, half, q] = copy(stage.at[i, 2 * half + q], xr.at[plane + 1], at_s.at[i, 2 * half + q],
                                         at_r.at[plane], at(x, y, q, zo(way_z * dist(i))))

    def work(i, half):
        project(i, half, from_gather(i))
        for q in range(2):
            tiles[i, half, q].start()

    def work_own(half, plane):
        project(2, half, from_own)
        tiles[2, half, 0].start()
        xr[plane + 1] = stage[2, 2 * half + 1]

    def third(body):
        pl.when(r == 0)(body)

    z_start(0)
    z_start(1)
    third(lambda: z_start(2))
    tok_near.start()
    small(0)
    tok_pair.start()
    large(0)
    small(1)
    third(lambda: small(2))
    large(1)
    third(lambda: large(2))
    tok_near.wait_recv()
    gathered(0)
    work(0, 0)
    tok_pair.wait_recv()
    tok_relay.start()
    tok_relay.wait_recv()
    work(0, 1)
    gathered(1)
    work(1, 0)
    work(1, 1)

    @pl.when(r == 0)
    def _():
        gathered(2)
        work(2, 0)
        work(2, 1)

    @pl.when(r == 1)
    def _():
        work_own(0, z)
        work_own(1, zpair)

    def tile_in(t):
        @pl.when(jnp.logical_or(r == 0, z // 2 != t // 2))
        def _():
            copy(stage.at[0, 0], xr.at[t + 1], at_s.at[0, 0], at_r.at[t], partner).wait_recv()

    def halo(dev):
        return copy(xr.at[NZ], xr.at[0], h_s, h_r, (dev, z))

    lane = lax.broadcasted_iota(jnp.int32, (WIDTH, TILE), 1)
    quad = 1.0 / (2.0 ** 0.5 * FEAT ** 0.5)
    one_row = jnp.where(lax.broadcasted_iota(jnp.int32, (8, TILE), 0) == 0, 1.0, 0.0)

    def features(u, twice):
        parts = [u * u * quad]
        for d in range(1, 8):
            parts.append(u * pltpu.roll(u, FEAT - d, 0) * (quad * twice))
        parts.append((u * pltpu.roll(u, 8, 0) * (quad * twice))[:8])
        parts.append(u * FEAT ** -0.25)
        parts.append(one_row)
        return jnp.concatenate(parts, axis=0)

    def convolve(t):
        before = xr[t].astype(f32)
        now = xr[t + 1].astype(f32)
        acc = cw[0] * now
        for o in range(1, 4):
            acc = acc + cw[o] * pltpu.roll(jnp.where(lane >= TILE - o, before, now), o, 1)
        vt[t] = acc[2 * FEAT:].astype(bf16)
        rows = pl.ds(t * TILE if isinstance(t, int) else pl.multiple_of(t * TILE, TILE), TILE)
        fq[rows, :] = features(acc[0:FEAT], 2.0).T.astype(bf16)
        fk[t] = features(acc[FEAT:2 * FEAT], 1.0).astype(bf16)

    a = 2 * (z // 2 + 2 + zpar)
    for pairs, ready in (((0, 1), (1, 2, 3)), ((-1, 2), (-1, 0, 4, 5)), ((-2, 3), (-4, -3, -2, 6, 7))):
        here = [lax.rem(a + 2 * p + q + NZ, NZ) for p in pairs for q in range(2)]
        for t in here:
            tile_in(t)

        @pl.when(jnp.logical_and(c < 2 * NX * NY - 1, jnp.logical_or(here[1] == NZ - 1, here[3] == NZ - 1)))
        def _():
            halo(c + 1).start()

        for n in ready:
            t = lax.rem(a + n + NZ, NZ)

            @pl.when(t != 0)
            def _():
                convolve(t)

    @pl.when(c == 0)
    def _():
        xr[0] = jnp.zeros((WIDTH, TILE), bf16)

    @pl.when(c > 0)
    def _():
        halo(c - 1).wait_recv()

    convolve(0)

    per = BLOCK // TILE

    def lanes(ref, b, n):
        return jnp.concatenate([ref[b * per + t] for t in range(n)], axis=1)

    ones = jnp.ones((8, BLOCK), bf16)
    for b in range(2):
        keys = lanes(fk, b, per)
        st[b] = dot_nt(keys, lanes(vt, b, per))
        total = dot_nt(ones, keys)
        st[b, TOT:TOT + 1, :] = total[0:1, 0:128]
        st[b, TOT + 1:TOT + 2, 0:32] = total[0:1, 128:160]
    loc[...] = st[0] + st[1]

    mine = pl.ds(pl.multiple_of(r * HALF, 8), HALF)
    other = pl.ds(pl.multiple_of((1 - r) * HALF, 8), HALF)
    d1 = copy(loc.at[other, :], px, d1_s, d1_r, partner)
    d1.start()
    sends.append(d1)

    def within(b):
        for i in range(BLOCK // SUB):
            cols = (i + 1) * SUB
            keys = lanes(fk, b, cols // TILE)
            row = b * BLOCK + i * SUB
            w = jnp.dot(fq[row:row + SUB, :], keys, preferred_element_type=f32)
            causal = (lax.broadcasted_iota(jnp.int32, (SUB, cols), 0) + i * SUB
                      >= lax.broadcasted_iota(jnp.int32, (SUB, cols), 1))
            w = jnp.where(causal, w, 0.0)
            num[row:row + SUB, :] = dot_nt(w.astype(bf16), lanes(vt, b, cols // TILE))
            den[row:row + SUB, :] = jnp.broadcast_to(jnp.sum(w, axis=1, keepdims=True), (SUB, 128))

    d1.wait_recv()
    chip = loc[mine, :] + px[...]
    ch[0] = chip[:PART]
    ch[1] = chip[PART:]

    def to_y(src, dst, ss, rs):
        out = []
        for d in range(1, NY):
            cp = copy(src(d), dst.at[d - 1], ss.at[d - 1], rs.at[d - 1], at(x, yo(d), r, z))
            cp.start()
            out.append(cp)
        sends.extend(out)
        return out

    x_sends = []

    def to_x(src, dst, ss, rs):
        out = []
        for d in range(1, NX):
            cp = copy(src, dst.at[d - 1], ss.at[d - 1], rs.at[d - 1], at(xo(d), y, r, z))
            pl.when(x + d < NX)(cp.start)
            out.append(cp)
            x_sends.append((d, cp))
        return out

    x_second = to_x(ch.at[1], xbuf.at[1], sx_s.at[1], sx_r.at[1])
    y_first = to_y(lambda d: ch.at[0], ybuf.at[0], sy_s.at[0], sy_r.at[0])
    within(0)
    second = jnp.zeros((PART, 128), f32)
    for d in range(1, NX):
        pl.when(x >= d)(x_second[d - 1].wait_recv)
        second = second + jnp.where(x >= d, xbuf[1, d - 1], 0.0)
    pb[0] = second
    pb[1] = second + ch[1]
    y_second = to_y(lambda d: pb.at[1 - (y + d) // NY], ybuf.at[1], sy_s.at[1], sy_r.at[1])
    within(1)
    total = ch[0]
    first_rows = jnp.zeros((PART, 128), f32)
    for d in range(1, NY):
        y_first[d - 1].wait_recv()
        got = ybuf[0, d - 1]
        total = total + got
        first_rows = first_rows + jnp.where(y >= d, got, 0.0)
    tx[...] = total
    x_first = to_x(tx, xbuf.at[0], sx_s.at[0], sx_r.at[0])
    for d in range(1, NY):
        y_second[d - 1].wait_recv()
        second = second + ybuf[1, d - 1]
    for d in range(1, NX):
        pl.when(x >= d)(x_first[d - 1].wait_recv)
        first_rows = first_rows + jnp.where(x >= d, xbuf[0, d - 1], 0.0)
    before = jnp.concatenate([first_rows, second], axis=0)
    snd[...] = before + jnp.where(r == 0, loc[mine, :], 0.0)
    d2 = copy(snd, fin.at[mine, :], d2_s, d2_r, partner)
    d2.start()
    sends.append(d2)
    fin[mine, :] = before + jnp.where(r == 1, px[...], 0.0)
    d2.wait_recv()

    for b in range(2):
        state = fin[...] if b == 0 else fin[...] + st[0]
        high = state.astype(bf16)
        low = (state - high.astype(f32)).astype(bf16)
        row = jnp.concatenate([state[TOT:TOT + 1, :], state[TOT + 1:TOT + 2, 0:32]], axis=1)
        row_high = row.astype(bf16).astype(f32)
        which = lax.broadcasted_iota(jnp.int32, (16, PHI), 0)
        rows = jnp.where(which == 0, row_high, jnp.where(which == 1, row - row_high, 0.0)).astype(bf16)
        for i in range(BLOCK // SUB):
            at_rows = slice(b * BLOCK + i * SUB, b * BLOCK + (i + 1) * SUB)
            f = fq[at_rows, :]
            top = num[at_rows, :] + jnp.dot(f, high, preferred_element_type=f32)
            top = top + jnp.dot(f, low, preferred_element_type=f32)
            two = dot_nt(f, rows)
            bottom = den[at_rows, :] + (two[:, 0:1] + two[:, 1:2])
            out_ref[at_rows, :] = (top / bottom).astype(bf16)

    def left(i):
        zr[i].wait_send()
        zx[i].wait_send()
        yb[i].wait_send()
        for dx in range(1, NX):
            xb[i, dx].wait_send()
        for dy in range(1, NY):
            ya[i, dy].wait_send()
        for half in range(2):
            tiles[i, half, 1].wait_send()

    for i in range(3):
        guard(i, lambda i=i: left(i))
        for half in range(2):
            tiles[i, half, 0].wait_send()
    for cp in (tok_near, tok_pair, tok_relay):
        cp.wait_send()
    for cp in sends:
        cp.wait_send()
    for d, cp in x_sends:
        pl.when(x + d < NX)(cp.wait_send)

    @pl.when(c < 2 * NX * NY - 1)
    def _():
        halo(c + 1).wait_send()


def per_device(tokens, projection, conv_weight):
    vmem = pltpu.VMEM
    dma = pltpu.SemaphoreType.DMA
    return pl.pallas_call(
        kernel,
        out_shape=jax.ShapeDtypeStruct((ROWS, VW), bf16),
        in_specs=[pl.BlockSpec(memory_space=pl.ANY)] * 3,
        out_specs=pl.BlockSpec(memory_space=vmem),
        scratch_shapes=[
            vmem((WIDTH, D), bf16),
            vmem((4, WIDTH), f32),
            dma((3,)),
            vmem((4, TILE, D), bf16),
            vmem((3, KY // 128, WIDTH, 128), bf16),
            vmem((3, NX, WIDTH, KX), bf16),
            vmem((3, 4, WIDTH, TILE), bf16),
            vmem((NZ + 1, WIDTH, TILE), bf16),
            vmem((4, WIDTH, TILE), f32),
            vmem((NZ, VW, TILE), bf16),
            vmem((ROWS, PHI), bf16),
            vmem((NZ, PHI, TILE), bf16),
            vmem((2, PHI, 128), f32),
            vmem((PHI, 128), f32),
            vmem((HALF, 128), f32),
            vmem((2, PART, 128), f32),
            vmem((2, NY - 1, PART, 128), f32),
            vmem((PART, 128), f32),
            vmem((2, NX - 1, PART, 128), f32),
            vmem((2, PART, 128), f32),
            vmem((HALF, 128), f32),
            vmem((PHI, 128), f32),
            vmem((ROWS, 128), f32),
            vmem((ROWS, 128), f32),
            dma((3,)), dma((3,)),
            dma((3,)), dma((3,)),
            dma((3,)), dma((3,)),
            dma((3, NY - 1)), dma((3, NY - 1)),
            dma((3,)), dma((3,)),
            dma((3, NX - 1)), dma((3, NX - 1)),
            dma((3, 4)), dma((NZ,)),
            dma, dma,
            dma, dma,
            dma((2, NY - 1)), dma((2, NY - 1)),
            dma((2, NX - 1)), dma((2, NX - 1)),
            dma, dma,
        ],
        compiler_params=pltpu.CompilerParams(
            collective_id=0, has_side_effects=True, vmem_limit_bytes=107 * 2**19),
        name="fused",
    )(tokens, projection.T, conv_weight)


def solution(mesh):
    return jax.shard_map(
        per_device,
        mesh=mesh,
        in_specs=(P(("ctx", "tp"), None), P(None, "tp"), P(None, "tp")),
        out_specs=P("ctx", "tp"),
        check_vma=False,
    )
```

```python
import jax
import jax.numpy as jnp
from jax import lax
from jax.experimental import pallas as pl
from jax.experimental.pallas import tpu as pltpu
from jax.sharding import PartitionSpec as P

NX, NY, NZ = 4, 8, 12
D = 2048
FEAT = 16
KY = D // 4
KX = (D - KY) // NX
VW = 128
WIDTH = 2 * FEAT + VW
TILE = 128
ROWS = TILE * NZ
PHI = 160
HALF = PHI // 2
PART = HALF // 2
TOT = 153
BLOCK = 768
SUB = 256
MESH = pl.DeviceIdType.MESH
bf16, f32 = jnp.bfloat16, jnp.float32


def dot_nt(a, b):
    return lax.dot_general(a, b, (((1,), (1,)), ((), ())), preferred_element_type=f32)


def kernel(tok_ref, proj_ref, conv_ref, out_ref,
           own_w, taps, in_sem, tokbuf, wr, wx, stage, xr, cw, vt, fq, fk, st, loc, px, ch, ybuf, tx, xbuf, pb, snd, fin, num, den,
           tk_s, tk_r, zr_s, zr_r, zx_s, zx_r, ya_s, ya_r, yb_s, yb_r, xb_s, xb_r, at_s, at_r, h_s, h_r,
           d1_s, d1_r, sy_s, sy_r, sx_s, sx_r, d2_s, d2_r):
    c = lax.axis_index("ctx")
    z = lax.axis_index("tp")
    r = lax.rem(c, 2)
    y = lax.rem(c // 2, NY)
    x = c // (2 * NY)
    ypar = lax.rem(y, 2)
    zpar = lax.rem(z, 2)

    def at(xx, yy, rr, zz):
        return ((xx * NY + yy) * 2 + rr, zz)

    def xo(d):
        return lax.rem(x + d + NX, NX)

    def yo(d):
        return lax.rem(y + d + NY, NY)

    def zo(d):
        return lax.rem(z + d + NZ, NZ)

    def copy(src, dst, ss, rs, dev):
        return pltpu.make_async_remote_copy(
            src_ref=src, dst_ref=dst, send_sem=ss, recv_sem=rs, device_id=dev, device_id_type=MESH)

    load_tok = pltpu.make_async_copy(tok_ref, tokbuf.at[zpar * 2 + r], in_sem.at[0])
    load_w = pltpu.make_async_copy(proj_ref, own_w, in_sem.at[1])
    load_taps = pltpu.make_async_copy(conv_ref, taps, in_sem.at[2])
    load_tok.start()
    load_w.start()
    load_taps.start()

    barrier = pltpu.get_barrier_semaphore()

    def greet(dev):
        pl.semaphore_signal(barrier, inc=1, device_id=dev, device_id_type=MESH)

    greet(at(x, y, 1 - r, z))
    for d in range(1, NX):
        greet(at(xo(d), y, r, z))
    for d in range(1, NY):
        greet(at(x, yo(d), r, z))
    for d in range(1, NZ):
        greet(at(x, y, r, zo(d)))
        greet(at(x, y, 1 - r, zo(d)))

    @pl.when(jnp.logical_and(r == 0, c > 0))
    def _():
        greet((c - 1, z))

    load_tok.wait()
    load_w.wait()
    load_taps.wait()
    ca = taps[...]
    ca = jnp.concatenate([ca, ca], axis=0)
    taps_qk = ca[:, 0:128].T
    taps_v = ca[:, 32:WIDTH].T
    for o in range(4):
        cw[o, 0:32] = jnp.broadcast_to(taps_qk[0:32, o:o + 1], (32, 128))
        cw[o, 32:] = jnp.broadcast_to(taps_v[:, o:o + 1], (VW, 128))

    pl.semaphore_wait(barrier, NX + NY - 1 + 2 * (NZ - 1) + r * (1 - c // (2 * NX * NY - 1)))

    way_z = 2 * zpar - 1
    sends = []

    def guard(i, body):
        if i == 2:
            pl.when(r == 0)(body)
        else:
            body()

    def dist(i):
        return 5 - r - 2 * i

    zpair = z - way_z
    partner = at(x, y, 1 - r, z)
    own_tok = tokbuf.at[zpar * 2 + r]
    far_tok = tokbuf.at[(1 - zpar) * 2 + r]
    tok_near = copy(own_tok, own_tok, tk_s.at[0], tk_r.at[0], partner)
    tok_pair = copy(own_tok, own_tok, tk_s.at[1], tk_r.at[1], at(x, y, r, zpair))
    tok_relay = copy(far_tok, far_tok, tk_s.at[2], tk_r.at[2], partner)

    rows = pl.ds(pl.multiple_of(ypar * 80, 16), 80)
    xlanes = pl.ds(pl.multiple_of(KY + x * KX, 128), KX)
    zr, zx, yb, ya, xb = {}, {}, {}, {}, {}
    for i in range(3):
        d = dist(i)
        to = at(x, y, r, zo(d * (1 - 2 * lax.rem(z + d, 2))))
        block = wr.at[i, y // 2, rows, :]
        zr[i] = copy(own_w.at[rows, pl.ds(pl.multiple_of(y // 2 * 128, 128), 128)], block, zr_s.at[i], zr_r.at[i], to)
        for dy in range(1, NY):
            ya[i, dy] = copy(block, block, ya_s.at[i, dy - 1], ya_r.at[i, dy - 1], at(x, yo(dy), r, z))
        block = wx.at[i, x, rows, :]
        zx[i] = copy(own_w.at[rows, xlanes], block, zx_s.at[i], zx_r.at[i], to)
        yb[i] = copy(block, block, yb_s.at[i], yb_r.at[i], at(x, y + 1 - 2 * ypar, r, z))
        block = wx.at[i, x]
        for dx in range(1, NX):
            xb[i, dx] = copy(block, block, xb_s.at[i, dx - 1], xb_r.at[i, dx - 1], at(xo(dx), y, r, z))

    def z_start(i):
        zr[i].start()
        zx[i].start()

    def small(i):
        zx[i].wait_recv()
        yb[i].start()
        zr[i].wait_recv()
        for dy in (4, 3, 5, 2, 6, 1, 7):
            ya[i, dy].start()

    def large(i):
        yb[i].wait_recv()
        for dx in (2, 1, 3):
            xb[i, dx].start()

    def gathered(i):
        for dx in range(1, NX):
            xb[i, dx].wait_recv()
        for dy in range(1, NY):
            ya[i, dy].wait_recv()

    def project(i, half, block):
        first_set = 2 * (zpar if half == 0 else 1 - zpar)
        acc = jnp.zeros((WIDTH, 2 * TILE), f32)
        for j in range(6):
            k = slice(j * 256, (j + 1) * 256) if j < 2 else slice(KY + (j - 2) * KX, KY + (j - 1) * KX)
            acc = acc + dot_nt(block(j, k), tokbuf[pl.ds(first_set, 2), :, k].reshape(2 * TILE, k.stop - k.start))
        for q in range(2):
            stage[i, 2 * half + q] = acc[:, q * TILE:(q + 1) * TILE].astype(bf16)

    def from_gather(i):
        def block(j, k):
            if j < 2:
                return jnp.concatenate([wr[i, 2 * j], wr[i, 2 * j + 1]], axis=1)
            return wx[i, j - 2]
        return block

    def from_own(j, k):
        return own_w[:, k]

    tiles = {}
    for i in range(3):
        for half, plane in ((0, z), (1, zpair)):
            for q in range(2):
                tiles[i, half, q] = copy(stage.at[i, 2 * half + q], xr.at[plane + 1], at_s.at[i, 2 * half + q],
                                         at_r.at[plane], at(x, y, q, zo(way_z * dist(i))))

    def work(i, half):
        project(i, half, from_gather(i))
        for q in range(2):
            tiles[i, half, q].start()

    def work_own(half, plane):
        project(2, half, from_own)
        tiles[2, half, 0].start()
        xr[plane + 1] = stage[2, 2 * half + 1]

    def third(body):
        pl.when(r == 0)(body)

    z_start(0)
    z_start(1)
    third(lambda: z_start(2))
    tok_near.start()
    small(0)
    tok_pair.start()
    large(0)
    small(1)
    third(lambda: small(2))
    large(1)
    third(lambda: large(2))
    tok_near.wait_recv()
    gathered(0)
    work(0, 0)
    tok_pair.wait_recv()
    tok_relay.start()
    tok_relay.wait_recv()
    work(0, 1)
    gathered(1)
    work(1, 0)
    work(1, 1)

    @pl.when(r == 0)
    def _():
        gathered(2)
        work(2, 0)
        work(2, 1)

    @pl.when(r == 1)
    def _():
        work_own(0, z)
        work_own(1, zpair)

    def tile_in(t):
        @pl.when(jnp.logical_or(r == 0, z // 2 != t // 2))
        def _():
            copy(stage.at[0, 0], xr.at[t + 1], at_s.at[0, 0], at_r.at[t], partner).wait_recv()

    def halo(dev):
        return copy(xr.at[NZ], xr.at[0], h_s, h_r, (dev, z))

    lane = lax.broadcasted_iota(jnp.int32, (WIDTH, TILE), 1)
    quad = 1.0 / (2.0 ** 0.5 * FEAT ** 0.5)
    one_row = jnp.where(lax.broadcasted_iota(jnp.int32, (8, TILE), 0) == 0, 1.0, 0.0)

    def features(u, twice):
        parts = [u * u * quad]
        for d in range(1, 8):
            parts.append(u * pltpu.roll(u, FEAT - d, 0) * (quad * twice))
        parts.append((u * pltpu.roll(u, 8, 0) * (quad * twice))[:8])
        parts.append(u * FEAT ** -0.25)
        parts.append(one_row)
        return jnp.concatenate(parts, axis=0)

    def convolve(t):
        before = xr[t].astype(f32)
        now = xr[t + 1].astype(f32)
        acc = cw[0] * now
        for o in range(1, 4):
            acc = acc + cw[o] * pltpu.roll(jnp.where(lane >= TILE - o, before, now), o, 1)
        vt[t] = acc[2 * FEAT:].astype(bf16)
        rows = pl.ds(t * TILE if isinstance(t, int) else pl.multiple_of(t * TILE, TILE), TILE)
        fq[rows, :] = features(acc[0:FEAT], 2.0).T.astype(bf16)
        fk[t] = features(acc[FEAT:2 * FEAT], 1.0).astype(bf16)

    a = 2 * (z // 2 + 2 + zpar)
    for pairs, ready in (((0, 1), (1, 2, 3)), ((-1, 2), (-1, 0, 4, 5)), ((-2, 3), (-4, -3, -2, 6, 7))):
        here = [lax.rem(a + 2 * p + q + NZ, NZ) for p in pairs for q in range(2)]
        for t in here:
            tile_in(t)

        @pl.when(jnp.logical_and(c < 2 * NX * NY - 1, jnp.logical_or(here[1] == NZ - 1, here[3] == NZ - 1)))
        def _():
            halo(c + 1).start()

        for n in ready:
            t = lax.rem(a + n + NZ, NZ)

            @pl.when(t != 0)
            def _():
                convolve(t)

    @pl.when(c == 0)
    def _():
        xr[0] = jnp.zeros((WIDTH, TILE), bf16)

    @pl.when(c > 0)
    def _():
        halo(c - 1).wait_recv()

    convolve(0)

    per = BLOCK // TILE

    def lanes(ref, b, n):
        return jnp.concatenate([ref[b * per + t] for t in range(n)], axis=1)

    ones = jnp.ones((8, BLOCK), bf16)
    for b in range(2):
        keys = lanes(fk, b, per)
        st[b] = dot_nt(keys, lanes(vt, b, per))
        total = dot_nt(ones, keys)
        st[b, TOT:TOT + 1, :] = total[0:1, 0:128]
        st[b, TOT + 1:TOT + 2, 0:32] = total[0:1, 128:160]
    loc[...] = st[0] + st[1]

    mine = pl.ds(pl.multiple_of(r * HALF, 8), HALF)
    other = pl.ds(pl.multiple_of((1 - r) * HALF, 8), HALF)
    d1 = copy(loc.at[other, :], px, d1_s, d1_r, partner)
    d1.start()
    sends.append(d1)

    def within(b):
        for i in range(BLOCK // SUB):
            cols = (i + 1) * SUB
            keys = lanes(fk, b, cols // TILE)
            row = b * BLOCK + i * SUB
            w = jnp.dot(fq[row:row + SUB, :], keys, preferred_element_type=f32)
            causal = (lax.broadcasted_iota(jnp.int32, (SUB, cols), 0) + i * SUB
                      >= lax.broadcasted_iota(jnp.int32, (SUB, cols), 1))
            w = jnp.where(causal, w, 0.0)
            num[row:row + SUB, :] = dot_nt(w.astype(bf16), lanes(vt, b, cols // TILE))
            den[row:row + SUB, :] = jnp.broadcast_to(jnp.sum(w, axis=1, keepdims=True), (SUB, 128))

    d1.wait_recv()
    chip = loc[mine, :] + px[...]
    ch[0] = chip[:PART]
    ch[1] = chip[PART:]

    def to_y(src, dst, ss, rs):
        out = []
        for d in range(1, NY):
            out.append(copy(src(d), dst.at[d - 1], ss.at[d - 1], rs.at[d - 1], at(x, yo(d), r, z)))
        for d in (4, 3, 5, 2, 6, 1, 7):
            out[d - 1].start()
        sends.extend(out)
        return out

    x_sends = []

    def to_x(src, dst, ss, rs):
        out = []
        for d in range(1, NX):
            cp = copy(src, dst.at[d - 1], ss.at[d - 1], rs.at[d - 1], at(xo(d), y, r, z))
            pl.when(x + d < NX)(cp.start)
            out.append(cp)
            x_sends.append((d, cp))
        return out

    y_first = to_y(lambda d: ch.at[0], ybuf.at[0], sy_s.at[0], sy_r.at[0])
    x_second = to_x(ch.at[1], xbuf.at[1], sx_s.at[1], sx_r.at[1])
    within(0)
    second = jnp.zeros((PART, 128), f32)
    for d in range(1, NX):
        pl.when(x >= d)(x_second[d - 1].wait_recv)
        second = second + jnp.where(x >= d, xbuf[1, d - 1], 0.0)
    pb[0] = second
    pb[1] = second + ch[1]
    y_second = to_y(lambda d: pb.at[1 - (y + d) // NY], ybuf.at[1], sy_s.at[1], sy_r.at[1])
    within(1)
    total = ch[0]
    first_rows = jnp.zeros((PART, 128), f32)
    for d in range(1, NY):
        y_first[d - 1].wait_recv()
        got = ybuf[0, d - 1]
        total = total + got
        first_rows = first_rows + jnp.where(y >= d, got, 0.0)
    tx[...] = total
    x_first = to_x(tx, xbuf.at[0], sx_s.at[0], sx_r.at[0])
    for d in range(1, NY):
        y_second[d - 1].wait_recv()
        second = second + ybuf[1, d - 1]
    for d in range(1, NX):
        pl.when(x >= d)(x_first[d - 1].wait_recv)
        first_rows = first_rows + jnp.where(x >= d, xbuf[0, d - 1], 0.0)
    before = jnp.concatenate([first_rows, second], axis=0)
    snd[...] = before + jnp.where(r == 0, loc[mine, :], 0.0)
    d2 = copy(snd, fin.at[mine, :], d2_s, d2_r, partner)
    d2.start()
    sends.append(d2)
    fin[mine, :] = before + jnp.where(r == 1, px[...], 0.0)
    d2.wait_recv()

    for b in range(2):
        state = fin[...] if b == 0 else fin[...] + st[0]
        high = state.astype(bf16)
        low = (state - high.astype(f32)).astype(bf16)
        row = jnp.concatenate([state[TOT:TOT + 1, :], state[TOT + 1:TOT + 2, 0:32]], axis=1)
        row_high = row.astype(bf16).astype(f32)
        which = lax.broadcasted_iota(jnp.int32, (16, PHI), 0)
        rows = jnp.where(which == 0, row_high, jnp.where(which == 1, row - row_high, 0.0)).astype(bf16)
        for i in range(BLOCK // SUB):
            at_rows = slice(b * BLOCK + i * SUB, b * BLOCK + (i + 1) * SUB)
            f = fq[at_rows, :]
            top = num[at_rows, :] + jnp.dot(f, high, preferred_element_type=f32)
            top = top + jnp.dot(f, low, preferred_element_type=f32)
            two = dot_nt(f, rows)
            bottom = den[at_rows, :] + (two[:, 0:1] + two[:, 1:2])
            out_ref[at_rows, :] = (top / bottom).astype(bf16)

    def left(i):
        zr[i].wait_send()
        zx[i].wait_send()
        yb[i].wait_send()
        for dx in range(1, NX):
            xb[i, dx].wait_send()
        for dy in range(1, NY):
            ya[i, dy].wait_send()
        for half in range(2):
            tiles[i, half, 1].wait_send()

    for i in range(3):
        guard(i, lambda i=i: left(i))
        for half in range(2):
            tiles[i, half, 0].wait_send()
    for cp in (tok_near, tok_pair, tok_relay):
        cp.wait_send()
    for cp in sends:
        cp.wait_send()
    for d, cp in x_sends:
        pl.when(x + d < NX)(cp.wait_send)

    @pl.when(c < 2 * NX * NY - 1)
    def _():
        halo(c + 1).wait_send()


def per_device(tokens, projection, conv_weight):
    vmem = pltpu.VMEM
    dma = pltpu.SemaphoreType.DMA
    return pl.pallas_call(
        kernel,
        out_shape=jax.ShapeDtypeStruct((ROWS, VW), bf16),
        in_specs=[pl.BlockSpec(memory_space=pl.ANY)] * 3,
        out_specs=pl.BlockSpec(memory_space=vmem),
        scratch_shapes=[
            vmem((WIDTH, D), bf16),
            vmem((4, WIDTH), f32),
            dma((3,)),
            vmem((4, TILE, D), bf16),
            vmem((3, KY // 128, WIDTH, 128), bf16),
            vmem((3, NX, WIDTH, KX), bf16),
            vmem((3, 4, WIDTH, TILE), bf16),
            vmem((NZ + 1, WIDTH, TILE), bf16),
            vmem((4, WIDTH, TILE), f32),
            vmem((NZ, VW, TILE), bf16),
            vmem((ROWS, PHI), bf16),
            vmem((NZ, PHI, TILE), bf16),
            vmem((2, PHI, 128), f32),
            vmem((PHI, 128), f32),
            vmem((HALF, 128), f32),
            vmem((2, PART, 128), f32),
            vmem((2, NY - 1, PART, 128), f32),
            vmem((PART, 128), f32),
            vmem((2, NX - 1, PART, 128), f32),
            vmem((2, PART, 128), f32),
            vmem((HALF, 128), f32),
            vmem((PHI, 128), f32),
            vmem((ROWS, 128), f32),
            vmem((ROWS, 128), f32),
            dma((3,)), dma((3,)),
            dma((3,)), dma((3,)),
            dma((3,)), dma((3,)),
            dma((3, NY - 1)), dma((3, NY - 1)),
            dma((3,)), dma((3,)),
            dma((3, NX - 1)), dma((3, NX - 1)),
            dma((3, 4)), dma((NZ,)),
            dma, dma,
            dma, dma,
            dma((2, NY - 1)), dma((2, NY - 1)),
            dma((2, NX - 1)), dma((2, NX - 1)),
            dma, dma,
        ],
        compiler_params=pltpu.CompilerParams(
            collective_id=0, has_side_effects=True, vmem_limit_bytes=107 * 2**19),
        name="fused",
    )(tokens, projection.T, conv_weight)


def solution(mesh):
    return jax.shard_map(
        per_device,
        mesh=mesh,
        in_specs=(P(("ctx", "tp"), None), P(None, "tp"), P(None, "tp")),
        out_specs=P("ctx", "tp"),
        check_vma=False,
    )
```
